128 devices in a mesh: dp: 16 (over z, y), tensor: 8 (over x, core).
Axes of the slice: x: 4, y: 4, z: 4, core: 2. Of those that a mesh axis runs over, the one named last changes fastest.
Arguments:
- attention: bfloat16 [4096, 8192], P('dp', 'tensor'), may hold values from -6 to 6
- residual: bfloat16 [4096, 8192], P('dp', 'tensor'), may hold values from -6 to 6
- out_proj: bfloat16 [8192, 8192], P(None, 'tensor'), may hold values from -0.0625 to 0.0625
- norm_gain: bfloat16 [8192], P('tensor'), may hold values from 0.25 to 1.75
- cotangent: bfloat16 [4096, 8192], P('dp', 'tensor'), may hold values from -6 to 6
- rewards: float32 [64], P('dp'), may hold values from -8 to 8
- group_ids: int32 [64], P('dp'), may hold values from 0 to 3, as said below
- kept_flags: int32 [64], P('dp'), may hold values 0 or 1
- lengths: int32 [16, 4], P('dp'), may hold values from 1 to 128, 256 in all within a row
Outputs:
- grad_attention: bfloat16 [4096, 8192], P('dp', 'tensor')
- grad_out_proj: bfloat16 [8192, 8192], P('dp', 'tensor')
- grad_residual: bfloat16 [4096, 8192], P('dp', 'tensor')
- grad_gain: float32 [8192], P('tensor')
The draws below stay inside these ranges and needn't reach their ends.
Inputs may be any that keep to these rules, and one draw needn't show every extreme that they name: `lengths`: row d lists the sequences of dp index d; each row sums to 256. `group_ids`: every group is named by exactly 16 sequences.
All inputs are finite; a program needn't handle non-finite values. No bound on the sum of `kept_flags` on one device may be relied on, other than what follows from the above.
Results may differ from the reference program's by a relative error of at most 0.0049.
Values may be sent and summed in bfloat16 or wider, within the bound.
No kernel may reach another device: no remote copies, remote signals or barrier semaphores. Data moves between devices by JAX's collectives and lax.ppermute only.
A program may use at most 192 MiB of HBM per device.

```python
import math
import jax
import jax.numpy as jnp
import numpy as np
from jax import lax

D = 8192
TOK_DEV = 256
S_DEV = 4
HD = 8192
TOKENS = 4096
SEQS = 64
GROUPS = 4
N_DP = 16


def assign_groups(key):
    shuffled = jax.random.permutation(jax.random.fold_in(key, 11), SEQS)
    return (shuffled // 16).astype(jnp.int32)


def draw_group_ids(key, part):
    return assign_groups(key)


def draw_rewards(key, part):
    members = assign_groups(key)
    key = jax.random.fold_in(key, 7)
    rank_key, level_key, noise_key = jax.random.split(key, 3)
    ranking = jax.random.permutation(rank_key, GROUPS)
    quiet = ranking < (GROUPS + 2) // 3
    spread = jnp.where(quiet, 0.4, 2.0).astype(jnp.float32)
    levels = jax.random.uniform(level_key, (GROUPS,), jnp.float32, -1.5, 1.5)
    noise = jnp.clip(jax.random.normal(noise_key, (SEQS,), jnp.float32), -3.0, 3.0)
    return (levels[members] + spread[members] * noise).astype(jnp.float32)


def plant(values, own_key, smallest, high):
    longest = values.shape.index(max(values.shape))
    spots = []
    for shift in (0, 1):
        where = [jax.random.randint(jax.random.fold_in(own_key, axis), (), 0, length) for axis, length in enumerate(values.shape)]
        where[longest] = (where[longest] + shift) % values.shape[longest]
        spots.append(tuple(where))
    return values.at[spots[0]].set(smallest).at[spots[1]].set(high)


def with_spikes(array, key, source, target, parts, factor):
    def block_of(dim):
        return (jnp.arange(array.shape[dim]) // (array.shape[dim] // parts)).reshape((-1,) + (1,) * (array.ndim - 1 - dim))

    one_side = jax.random.permutation(key, parts)[block_of(target)]
    far = (block_of(target) + parts // 2) % parts
    return jnp.where((block_of(source) == one_side) | (block_of(source) == far), factor * array, array)


def level_of(rng, shape, pieces, least, top_value):
    gain, own = 1.0, jax.random.fold_in(rng, 6)
    for dim, blocks in pieces:
        steps = jnp.exp(jax.random.uniform(jax.random.fold_in(own, dim), (blocks,), jnp.float32, least / len(pieces), top_value / len(pieces)))
        gain = gain * jnp.repeat(steps, shape[dim] // blocks).reshape([-1 if axis == dim else 1 for axis in range(len(shape))])
    return gain


def split_up(count, total, most, skew):
    weights = [(1 << 20) // math.isqrt(grade ** skew) + 1 for grade in range(2, count + 1)]
    surplus, counts = total - most - (count - 1), [1] * (count - 1)
    while surplus > 0:
        movable = [i for i in range(count - 1) if counts[i] < most]
        pool, left = sum([weights[i] for i in movable]), surplus
        for i in movable:
            addition = min(most - counts[i], max(1, left * weights[i] // pool), surplus)
            counts[i] = counts[i] + addition
            surplus = surplus - addition
    return np.array([most] + counts)


def uneven(key, number_of, total, reach, slope):
    if number_of == 2:
        one = jax.random.randint(key, (), max(1, total - reach), min(reach, total - 1) + 1)
        return jnp.stack([one, total - one])
    sizes = jnp.asarray(split_up(number_of, total, reach, slope), jnp.int32)
    pairs = (number_of - 1) // 2
    giver, sink = sizes[1:1 + 2 * pairs:2], sizes[2:2 + 2 * pairs:2]
    margin = jnp.minimum(giver - 1, reach - sink)
    passed = jax.random.randint(jax.random.fold_in(key, 1), (pairs,), 0, 1 << 20) % (margin + 1)
    sizes = sizes.at[1:1 + 2 * pairs:2].set(giver - passed).at[2:2 + 2 * pairs:2].set(sink + passed)
    return sizes[jax.random.permutation(jax.random.fold_in(key, 2), number_of)]


def gaussian(rng, shape, deviation, most, cuts=(), kind=jnp.bfloat16):
    values = jax.random.normal(rng, shape, jnp.float32) * deviation
    if len(cuts) > 0:
        values = level_of(rng, shape, cuts, -0.22, 0.18) * values
    return jnp.clip(values, min=-most, max=most).astype(kind)


def noise_with(own_key, shape, scale, most, shards, heavy, kind=jnp.bfloat16):
    values = scale * jax.random.normal(own_key, shape, jnp.float32)
    if shards:
        values = values * level_of(own_key, shape, shards, -0.22, 0.18)
    return jnp.clip(with_spikes(values, jax.random.fold_in(own_key, 3), *heavy), -most, most).astype(kind)


def setup_inputs(seed: int = 0) -> dict:
    keys = jax.random.split(jax.random.key(seed), 10)
    attention = gaussian(keys[0], (TOKENS, HD), 1.0, 6.0, ((0, 16), (1, 8)))
    residual = gaussian(keys[1], (TOKENS, D), 1.0, 6.0, ((0, 16), (1, 8)))
    out_proj = gaussian(keys[2], (D, HD), HD ** -0.5, 0.0625, ((1, 8),))
    norm_gain = jnp.clip(1.0 + 0.15 * jax.random.normal(keys[3], (D,), jnp.float32), 0.25, 1.75).astype(jnp.bfloat16)
    cotangent = noise_with(keys[4], (TOKENS, D), 1.0, 6.0, ((0, 16), (1, 8)), (0, 1, 16, 2.0))
    rewards = draw_rewards(jax.random.fold_in(keys[9], 71), 0)
    group_ids = draw_group_ids(jax.random.fold_in(keys[9], 71), 0)
    kept_flags = plant((jax.random.randint(keys[7], (SEQS,), 0, 4) < 3).astype(jnp.int32), jax.random.fold_in(keys[7], 1), 0, 1)
    lengths = jax.vmap(lambda own: uneven(own, S_DEV, TOK_DEV, TOK_DEV // 2, 2))(jax.random.split(keys[8], N_DP)).reshape((N_DP, S_DEV)).astype(jnp.int32)
    return {"attention": attention, "residual": residual, "out_proj": out_proj, "norm_gain": norm_gain, "cotangent": cotangent, "rewards": rewards, "group_ids": group_ids, "kept_flags": kept_flags, "lengths": lengths}


def reference(attention, residual, out_proj, norm_gain, cotangent, rewards, group_ids, kept_flags, lengths):
    kept = kept_flags.astype(jnp.float32)
    onehot = (group_ids[None, :] == jnp.arange(GROUPS, dtype=jnp.int32)[:, None]).astype(jnp.float32)
    count = lax.optimization_barrier(jnp.sum(onehot * kept[None, :], axis=1))
    reward_sum = lax.optimization_barrier(jnp.sum(onehot * (kept * rewards)[None, :], axis=1))
    square_sum = lax.optimization_barrier(jnp.sum(onehot * (kept * rewards * rewards)[None, :], axis=1))
    kept_tokens = jnp.sum(kept * lengths.reshape(-1).astype(jnp.float32))
    group_mean = reward_sum / jnp.maximum(count, 1.0)
    group_var = square_sum / jnp.maximum(count, 1.0) - group_mean * group_mean
    group_scale = jnp.sqrt(jnp.maximum(group_var, 1.0))
    seq_mean = lax.optimization_barrier(jnp.sum(onehot * group_mean[:, None], axis=0))
    seq_scale = lax.optimization_barrier(jnp.sum(onehot * group_scale[:, None], axis=0))
    advantage = (rewards - seq_mean) / seq_scale
    seq_coef = -advantage * kept * float(TOKENS) / jnp.maximum(kept_tokens, 1.0)
    ends = jnp.cumsum(lengths, axis=1).astype(jnp.int32)
    position = jnp.arange(TOK_DEV, dtype=jnp.int32)
    segment = lax.optimization_barrier(jnp.sum((position[None, :, None] >= ends[:, None, :]).astype(jnp.int32), axis=2))
    picks = (segment[:, :, None] == jnp.arange(S_DEV, dtype=jnp.int32)[None, None, :]).astype(jnp.float32)
    token_coef = lax.optimization_barrier(jnp.sum(picks * seq_coef.reshape(N_DP, 1, S_DEV), axis=2)).reshape(TOKENS)
    upstream = token_coef[:, None] * cotangent.astype(jnp.float32)
    hidden = residual.astype(jnp.float32) + jnp.dot(attention, out_proj.T, preferred_element_type=jnp.float32)
    inverse = lax.rsqrt(lax.optimization_barrier(jnp.mean(hidden * hidden, axis=1)) + 1e-06)
    scaled = upstream * norm_gain.astype(jnp.float32)[None, :]
    inner = lax.optimization_barrier(jnp.mean(scaled * hidden, axis=1))
    grad_hidden = inverse[:, None] * scaled - hidden * (inverse * inverse * inverse * inner)[:, None]
    grad_residual = grad_hidden.astype(jnp.bfloat16)
    grad_gain = lax.optimization_barrier(jnp.sum(upstream * hidden * inverse[:, None], axis=0))
    grad_attention = jnp.dot(grad_residual, out_proj, preferred_element_type=jnp.float32).astype(jnp.bfloat16)
    grad_out_proj = jnp.dot(grad_residual.T, attention, preferred_element_type=jnp.float32).astype(jnp.bfloat16)
    return (grad_attention, grad_out_proj, grad_residual, grad_gain)
```

```python
import functools

import jax
import jax.numpy as jnp
from jax import lax
from jax.experimental import pallas as pl
from jax.experimental.pallas import tpu as pltpu
from jax.sharding import PartitionSpec as P

BF = jnp.bfloat16
F32 = jnp.float32
LIMIT = 48 * 1024 * 1024
CORE_SWAP = [(t, t ^ 1) for t in range(8)]


def x_shift(k):
    return [(t, ((t // 2 + k) % 4) * 2 + t % 2) for t in range(8)]


def dp_shift(dz, dy):
    return [(d, ((d // 4 + dz) % 4) * 4 + (d % 4 + dy) % 4) for d in range(16)]


def plane_shift(stage, k):
    pairs = []
    for d in range(16):
        for t in range(8):
            z, y = d // 4, d % 4
            if (t % 2) == stage:
                z = (z + k) % 4
            else:
                y = (y + k) % 4
            pairs.append((d * 8 + t, (z * 4 + y) * 8 + t))
    return pairs


def swap(value):
    return lax.ppermute(value, "tensor", CORE_SWAP)


def params():
    return pltpu.CompilerParams(vmem_limit_bytes=LIMIT)


def partial_kernel(shifts, where, att, w, send, keep, buf, sems):
    x, c = where[2], where[3]
    step = buf.shape[1]
    count = 2 * len(shifts)

    def copy(n):
        i, own = n // 2, n % 2
        slot = i // 2
        shift = shifts[-1]
        for k in range(len(shifts) - 1):
            shift = jnp.where(slot == k, shifts[k], shift)
        piece = lax.rem(x + shift, 4) * 2 + jnp.where(own == 1, c, 1 - c)
        row = pl.multiple_of((piece * 2 + lax.rem(i, 2)) * step, step)
        return pltpu.make_async_copy(w.at[pl.ds(row, step)], buf.at[n], sems.at[n])

    @pl.loop(0, 2 * count)
    def _(n):
        copy(n).start()

    @pl.loop(0, count)
    def _(i):
        slot = i // 2
        columns = pl.ds(pl.multiple_of(lax.rem(i, 2) * step, step), step)
        dims = (((1,), (1,)), ((), ()))
        copy(2 * i).wait()
        send[slot, :, columns] = lax.dot_general(
            att[...], buf[2 * i], dims, preferred_element_type=F32
        ).astype(BF)
        copy(2 * i + 1).wait()
        keep[slot, :, columns] = lax.dot_general(
            att[...], buf[2 * i + 1], dims, preferred_element_type=F32
        )


def partial_products(where, attention, out_proj, shifts):
    rows, depth = attention.shape
    width = out_proj.shape[0] // 8
    step = width // 2
    slots = len(shifts)
    vmem = pl.BlockSpec(memory_space=pltpu.VMEM)
    return pl.pallas_call(
        functools.partial(partial_kernel, shifts),
        in_specs=[
            pl.BlockSpec(memory_space=pltpu.SMEM),
            vmem,
            pl.BlockSpec(memory_space=pl.ANY),
        ],
        out_specs=[vmem, vmem],
        out_shape=[
            jax.ShapeDtypeStruct((slots, rows, width), BF),
            jax.ShapeDtypeStruct((slots, rows, width), F32),
        ],
        scratch_shapes=[
            pltpu.VMEM((4 * slots, step, depth), BF),
            pltpu.SemaphoreType.DMA((4 * slots,)),
        ],
        compiler_params=params(),
        cost_estimate=pl.CostEstimate(
            flops=4 * slots * rows * depth * width,
            bytes_accessed=4 * slots * width * depth,
            transcendentals=0,
        ),
        name="partial",
    )(where, attention, out_proj)


def row_sums(value):
    rows, width = value.shape
    part = value[:, 0:128]
    for i in range(1, width // 128):
        part = part + value[:, i * 128 : (i + 1) * 128]
    return jnp.sum(part.T, axis=0, keepdims=True)


def hidden_kernel(keep, own, r1, r2, r3, residual, cot, gain, hidden, sums):
    h = keep[...] + own[...].astype(F32) + residual[...].astype(F32)
    h = h + r1[...].astype(F32) + r2[...].astype(F32) + r3[...].astype(F32)
    hidden[...] = h
    scaled = cot[...].astype(F32) * gain[...].astype(F32)
    first = row_sums(h * h)
    second = row_sums(scaled * h)
    sums[...] = jnp.concatenate([first, second, jnp.zeros((6, first.shape[1]), F32)], axis=0)


def hidden_call(keep, own, r1, r2, r3, residual, cot, gain):
    rows, width = keep.shape
    big = pl.BlockSpec((128, width), lambda i: (i, 0))
    return pl.pallas_call(
        hidden_kernel,
        grid=(rows // 128,),
        in_specs=[big] * 7 + [pl.BlockSpec((1, width), lambda i: (0, 0))],
        out_specs=[big, pl.BlockSpec((8, 128), lambda i: (0, i))],
        out_shape=[
            jax.ShapeDtypeStruct((rows, width), F32),
            jax.ShapeDtypeStruct((8, rows), F32),
        ],
        compiler_params=params(),
        cost_estimate=pl.CostEstimate(
            flops=12 * rows * width, bytes_accessed=20 * rows * width, transcendentals=0
        ),
        name="hidden",
    )(keep, own, r1, r2, r3, residual, cot, gain)


def column(row):
    return jnp.broadcast_to(row, (128, 128)).T


def spread(col, width):
    return jnp.concatenate([col] * (width // 128), axis=1)


def grad_kernel(features, hidden, cot, gain, s0, s1, s2, s3, coef, grad, gain_term):
    i = pl.program_id(0)
    width = hidden.shape[1]
    sums = s0[...] + s1[...] + s2[...] + s3[...]
    square, inner = sums[0:1, :], sums[1:2, :]
    inverse = lax.rsqrt(square / features + 1e-06)
    first = coef[...] * inverse
    second = coef[...] * (inverse * inverse * inverse * inner / features)
    first = spread(column(first), width)
    second = spread(column(second), width)
    h = hidden[...]
    c = cot[...].astype(F32)
    grad[...] = (first * (c * gain[...].astype(F32)) - h * second).astype(BF)
    term = jnp.sum(first * c * h, axis=0, keepdims=True)

    @pl.when(i == 0)
    def _():
        gain_term[...] = term

    @pl.when(i != 0)
    def _():
        gain_term[...] += term


def grad_call(features, hidden, cot, gain, s0, s1, s2, s3, coef):
    rows, width = hidden.shape
    big = pl.BlockSpec((128, width), lambda i: (i, 0))
    small = pl.BlockSpec((8, 128), lambda i: (0, i))
    return pl.pallas_call(
        functools.partial(grad_kernel, float(features)),
        grid=(rows // 128,),
        in_specs=[big, big, pl.BlockSpec((1, width), lambda i: (0, 0))]
        + [small] * 4
        + [pl.BlockSpec((1, 128), lambda i: (0, i))],
        out_specs=[big, pl.BlockSpec((1, width), lambda i: (0, 0))],
        out_shape=[
            jax.ShapeDtypeStruct((rows, width), BF),
            jax.ShapeDtypeStruct((1, width), F32),
        ],
        compiler_params=params(),
        cost_estimate=pl.CostEstimate(
            flops=12 * rows * width, bytes_accessed=8 * rows * width, transcendentals=0
        ),
        name="grad",
    )(hidden, cot, gain, s0, s1, s2, s3, coef)


def attention_kernel(where, *refs):
    pieces, w, out, buf, acc, sems = refs[:8], refs[8], refs[9], refs[10], refs[11], refs[12]
    x, c = where[2], where[3]
    step = buf.shape[1]
    copies = []
    for n in range(8):
        holder = (1 - c) if n % 2 else c
        piece = lax.rem(x + 4 - n // 2, 4) * 2 + holder
        row = pl.multiple_of(piece * step, step)
        copies.append(pltpu.make_async_copy(w.at[pl.ds(row, step)], buf.at[n], sems.at[n]))
        copies[-1].start()
    for n in range(8):
        copies[n].wait()
        term = jnp.dot(pieces[n][...], buf[n], preferred_element_type=F32)
        if n == 0:
            acc[...] = term
        elif n < 7:
            acc[...] += term
        else:
            out[...] = (acc[...] + term).astype(BF)


def attention_call(where, pieces, out_proj):
    rows, width = pieces[0].shape
    depth = out_proj.shape[1]
    vmem = pl.BlockSpec(memory_space=pltpu.VMEM)
    return pl.pallas_call(
        attention_kernel,
        in_specs=[pl.BlockSpec(memory_space=pltpu.SMEM)]
        + [vmem] * 8
        + [pl.BlockSpec(memory_space=pl.ANY)],
        out_specs=vmem,
        scratch_shapes=[
            pltpu.VMEM((8, width, depth), BF),
            pltpu.VMEM((rows, depth), F32),
            pltpu.SemaphoreType.DMA((8,)),
        ],
        out_shape=jax.ShapeDtypeStruct((rows, depth), BF),
        compiler_params=params(),
        cost_estimate=pl.CostEstimate(
            flops=2 * rows * depth * width * 8,
            bytes_accessed=2 * 8 * width * depth,
            transcendentals=0,
        ),
        name="attention_grad",
    )(where, *pieces, out_proj)


def first_pack_kernel(where, *refs):
    pieces, outs = refs[:8], refs[8:12]
    z, y, x, c = where[0], where[1], where[2], where[3]
    rows, half = outs[0].shape[1:]
    for k in range(4):
        big_z = lax.rem(x + 4 - k, 4)
        for other in range(2):
            holder = (1 - c) if other else c
            for h in range(2):
                big_y = 2 * holder + h
                slot = jnp.where(c == 0, lax.rem(big_z + 4 - z, 4), lax.rem(big_y + 4 - y, 4))
                j = jnp.where(c == 0, big_y, big_z)
                start = pl.multiple_of(h * 2 * half + c * half, half)
                for s in range(4):

                    @pl.when(slot == s)
                    def _(s=s, j=j, start=start, piece=pieces[k * 2 + other]):
                        @pl.loop(0, rows // 64)
                        def _(r):
                            band = pl.ds(pl.multiple_of(r * 64, 64), 64)
                            outs[s][j, band, :] = piece[band, pl.ds(start, half)]


def second_pack_kernel(where, *refs):
    parts, outs = refs[:4], refs[4:8]
    rows = outs[0].shape[1]
    mine = jnp.where(where[3] == 0, where[1], where[0])
    for u in range(4):
        j = lax.rem(mine + u, 4)
        for s in range(4):

            @pl.loop(0, rows // 64)
            def _(r, u=u, s=s, j=j):
                band = pl.ds(pl.multiple_of(r * 64, 64), 64)
                outs[u][s, band, :] = parts[s][j, band, :]


def pack_call(kernel, where, inputs, rows, half, name):
    vmem = pl.BlockSpec(memory_space=pltpu.VMEM)
    return pl.pallas_call(
        kernel,
        in_specs=[pl.BlockSpec(memory_space=pltpu.SMEM)] + [vmem] * len(inputs),
        out_specs=[vmem] * 4,
        out_shape=[jax.ShapeDtypeStruct((4, rows, half), BF)] * 4,
        compiler_params=pltpu.CompilerParams(vmem_limit_bytes=16 * 1024 * 1024),
        cost_estimate=pl.CostEstimate(
            flops=0, bytes_accessed=64 * rows * half, transcendentals=0
        ),
        name=name,
    )(where, *inputs)


def projection_kernel(members, first, last, where, *refs):
    count = len(members)
    mine, theirs = refs[:count], refs[count : 2 * count]
    refs = refs[2 * count :]
    gathered = refs[0]
    before = None if first else refs[1]
    out, buf, acc, sems = refs[1 if first else 2 :]
    z, y, c = where[0], where[1], where[3]
    rows = buf.shape[1]
    half = acc.shape[1]
    copies = []
    for m, u in enumerate(members):
        for s in range(4):
            for n in range(2):
                z_first = (c == 0) if n == 0 else (c == 1)
                dz, dy = jnp.where(z_first, s, u), jnp.where(z_first, u, s)
                row = lax.rem(z + 4 - dz, 4) * 4 + lax.rem(y + 4 - dy, 4)
                row = pl.multiple_of(row * rows, rows)
                i = len(copies)
                copies.append(
                    pltpu.make_async_copy(gathered.at[pl.ds(row, rows)], buf.at[i], sems.at[i])
                )
                copies[-1].start()
    i = 0
    for m in range(count):
        for s in range(4):
            for n, lhs in ((0, mine[m].at[s]), (1, theirs[m].at[s])):
                copies[i].wait()
                term = lax.dot_general(
                    lhs[...], buf[i], (((0,), (0,)), ((), ())), preferred_element_type=F32
                )
                if i >= 2:
                    acc[n] += term
                elif first:
                    acc[n] = term
                else:
                    acc[n] = before[n] + term
                i += 1
    if last:
        low = pl.multiple_of(c * half, half)
        high = pl.multiple_of((1 - c) * half, half)
        out[pl.ds(low, half), :] = acc[0].astype(BF)
        out[pl.ds(high, half), :] = acc[1].astype(BF)
    else:
        out[...] = acc[...]


def projection_call(where, mine, theirs, gathered, members, before, last):
    _, rows, half = mine[0].shape
    depth = gathered.shape[1]
    vmem = pl.BlockSpec(memory_space=pltpu.VMEM)
    blocks = 8 * len(members)
    picked = [mine[u] for u in members] + [theirs[u] for u in members]
    first = before is None
    return pl.pallas_call(
        functools.partial(projection_kernel, members, first, last),
        in_specs=[pl.BlockSpec(memory_space=pltpu.SMEM)]
        + [vmem] * len(picked)
        + [pl.BlockSpec(memory_space=pl.ANY)]
        + ([] if first else [vmem]),
        out_specs=vmem,
        scratch_shapes=[
            pltpu.VMEM((blocks, rows, depth), BF),
            pltpu.VMEM((2, half, depth), F32),
            pltpu.SemaphoreType.DMA((blocks,)),
        ],
        out_shape=jax.ShapeDtypeStruct((2 * half, depth), BF)
        if last
        else jax.ShapeDtypeStruct((2, half, depth), F32),
        compiler_params=params(),
        cost_estimate=pl.CostEstimate(
            flops=2 * blocks * rows * half * depth,
            bytes_accessed=2 * blocks * rows * (depth + half),
            transcendentals=0,
        ),
        name="projection_grad",
    )(where, *picked, gathered, *([] if first else [before]))


def dp_sum(value):
    total = value
    for k in range(1, 4):
        total = total + lax.ppermute(value, "dp", dp_shift(0, k))
    result = total
    for k in range(1, 4):
        result = result + lax.ppermute(total, "dp", dp_shift(k, 0))
    return result


def token_scaling(rewards, group_ids, kept_flags, lengths, rows):
    dp_count = lax.axis_size("dp")
    groups = rewards.shape[0] * dp_count // 16
    seqs_here = rewards.shape[0]
    kept = kept_flags.astype(F32)
    onehot = (group_ids[None, :] == jnp.arange(groups, dtype=jnp.int32)[:, None]).astype(F32)
    stats = jnp.stack(
        [
            jnp.sum(onehot * kept[None, :], axis=1),
            jnp.sum(onehot * (kept * rewards)[None, :], axis=1),
            jnp.sum(onehot * (kept * rewards * rewards)[None, :], axis=1),
        ]
    )
    local_tokens = jnp.sum(kept * lengths[0].astype(F32))
    packed = jnp.concatenate([stats, jnp.full((1, groups), local_tokens, F32)], axis=0)
    packed = dp_sum(packed)
    stats, kept_tokens = packed[:3], packed[3, 0]
    group_mean = stats[1] / jnp.maximum(stats[0], 1.0)
    group_var = stats[2] / jnp.maximum(stats[0], 1.0) - group_mean * group_mean
    group_scale = jnp.sqrt(jnp.maximum(group_var, 1.0))
    seq_mean = jnp.sum(onehot * group_mean[:, None], axis=0)
    seq_scale = jnp.sum(onehot * group_scale[:, None], axis=0)
    advantage = (rewards - seq_mean) / seq_scale
    seq_coef = -advantage * kept * float(rows * dp_count) / jnp.maximum(kept_tokens, 1.0)
    ends = jnp.cumsum(lengths[0])
    position = jnp.arange(rows, dtype=jnp.int32)
    segment = jnp.sum((position[:, None] >= ends[None, :]).astype(jnp.int32), axis=1)
    picks = (segment[:, None] == jnp.arange(seqs_here, dtype=jnp.int32)[None, :]).astype(F32)
    return jnp.sum(picks * seq_coef[None, :], axis=1)


def shards(
    attention, residual, out_proj, norm_gain, cotangent, rewards, group_ids, kept_flags, lengths
):
    rows = attention.shape[0]
    features = out_proj.shape[0]
    d, t = lax.axis_index("dp"), lax.axis_index("tensor")
    where = jnp.stack([d // 4, d % 4, t // 2, t % 2]).astype(jnp.int32)
    gain = norm_gain[None, :]

    gathered = lax.all_gather(attention, "dp", axis=0, tiled=True)

    arrived = {}
    send, keep = partial_products(where, attention, out_proj, (2,))
    both = (keep[0] + swap(send)[0].astype(F32)).astype(BF)
    arrived[2] = lax.ppermute(both, "tensor", x_shift(2))
    later_where, _ = lax.optimization_barrier((where, both))
    send, keep = partial_products(later_where, attention, out_proj, (1, 3, 0))
    sent = swap(send)
    for i, k in ((0, 1), (1, 3)):
        both = (keep[i] + sent[i].astype(F32)).astype(BF)
        arrived[k] = lax.ppermute(both, "tensor", x_shift(k))
    rewards, group_ids, kept_flags, lengths, _ = lax.optimization_barrier(
        (rewards, group_ids, kept_flags, lengths, both)
    )
    coef = token_scaling(rewards, group_ids, kept_flags, lengths, rows)
    residual, coef = lax.optimization_barrier((residual, coef))
    hidden, sums = hidden_call(
        keep[2], sent[2], arrived[1], arrived[2], arrived[3], residual, cotangent, gain
    )

    chip = sums + swap(sums)
    others = [lax.ppermute(chip, "tensor", x_shift(k)) for k in (1, 2, 3)]
    grad_residual, gain_term = grad_call(
        features, hidden, cotangent, gain, chip, *others, coef[None, :]
    )

    pieces = []
    for k in range(4):
        piece = grad_residual if k == 0 else lax.ppermute(grad_residual, "tensor", x_shift(k))
        pieces.extend([piece, swap(piece)])
    gain_term, _ = lax.optimization_barrier((gain_term, pieces[1]))
    grad_gain = dp_sum(gain_term)[0]

    half = features // 32
    pack_where, grad_gain = lax.optimization_barrier((where, grad_gain))
    sends = pack_call(first_pack_kernel, pack_where, pieces, rows, half, "first_pack")
    parts = [sends[0]] + [
        lax.ppermute(sends[k], ("dp", "tensor"), plane_shift(0, k)) for k in (1, 2, 3)
    ]
    late_where, _ = lax.optimization_barrier((where, sends))
    grad_attention = attention_call(late_where, pieces, out_proj)
    pack_where, _ = lax.optimization_barrier((where, grad_attention))
    sends = pack_call(second_pack_kernel, pack_where, parts, rows, half, "second_pack")
    mine = [sends[0]] + [
        lax.ppermute(sends[k], ("dp", "tensor"), plane_shift(1, k)) for k in (1, 2, 3)
    ]
    theirs = [swap(part) for part in mine]
    total = projection_call(where, mine, theirs, gathered, (0,), None, False)
    grad_out_proj = projection_call(where, mine, theirs, gathered, (1, 3, 2), total, True)
    return (grad_attention, grad_out_proj, grad_residual, grad_gain)


def solution(mesh):
    return jax.shard_map(
        shards,
        mesh=mesh,
        in_specs=(
            P("dp", "tensor"),
            P("dp", "tensor"),
            P(None, "tensor"),
            P("tensor"),
            P("dp", "tensor"),
            P("dp"),
            P("dp"),
            P("dp"),
            P("dp", None),
        ),
        out_specs=(P("dp", "tensor"), P("dp", "tensor"), P("dp", "tensor"), P("tensor")),
        check_vma=False,
    )
```

```python
import functools

import jax
import jax.numpy as jnp
from jax import lax
from jax.experimental import pallas as pl
from jax.experimental.pallas import tpu as pltpu
from jax.sharding import PartitionSpec as P

BF = jnp.bfloat16
F32 = jnp.float32
LIMIT = 48 * 1024 * 1024
EXTRA = 16
GROUPS = 4
CORE_SWAP = [(t, t ^ 1) for t in range(8)]


def x_shift(k):
    return [(t, ((t // 2 + k) % 4) * 2 + t % 2) for t in range(8)]


def plane_shift(stage, k):
    pairs = []
    for d in range(16):
        for t in range(8):
            z, y = d // 4, d % 4
            if (t % 2) == stage:
                z = (z + k) % 4
            else:
                y = (y + k) % 4
            pairs.append((d * 8 + t, (z * 4 + y) * 8 + t))
    return pairs


def scattered(step):
    return [(d * 8 + t, ((d + 2 * t + step) % 16) * 8 + t) for d in range(16) for t in range(8)]


def swap(value):
    return lax.ppermute(value, "tensor", CORE_SWAP)


def params():
    return pltpu.CompilerParams(vmem_limit_bytes=LIMIT)


def partial_kernel(jobs, where, attention, w, *refs):
    ins = sum(1 for job in jobs if job[2])
    got, outs = refs[:ins], refs[ins:-3]
    att, buf, sems = refs[-3:]
    x, c = where[2], where[3]
    step = buf.shape[1]
    copies = []
    for shift, other, _, _ in jobs:
        piece = lax.rem(x + shift, 4) * 2 + (1 - c if other else c)
        for h in range(2):
            row = pl.multiple_of((piece * 2 + h) * step, step)
            n = len(copies)
            copies.append(pltpu.make_async_copy(w.at[pl.ds(row, step)], buf.at[n], sems.at[n]))
    left = pltpu.make_async_copy(attention, att, sems.at[len(copies)])
    left.start()
    for copy in copies:
        copy.start()
    left.wait()
    used = 0
    for n, (_, _, add, _) in enumerate(jobs):
        if add:
            used += 1

        for h in range(2):
            copies[2 * n + h].wait()

        @pl.loop(0, 2)
        def _(h, n=n, add=add, used=used):
            columns = pl.ds(pl.multiple_of(h * step, step), step)
            term = lax.dot_general(
                att[...], buf[2 * n + h], (((1,), (1,)), ((), ())), preferred_element_type=F32
            )
            if add:
                term += got[used - 1][:, columns].astype(F32)
            outs[n][:, columns] = term.astype(outs[n].dtype)


def partial_products(where, attention, out_proj, jobs, got=()):
    rows, depth = attention.shape
    width = out_proj.shape[0] // 8
    step = width // 2
    count = 2 * len(jobs)
    vmem = pl.BlockSpec(memory_space=pltpu.VMEM)
    far = pl.BlockSpec(memory_space=pltpu.HBM)
    return pl.pallas_call(
        functools.partial(partial_kernel, jobs),
        in_specs=[pl.BlockSpec(memory_space=pltpu.SMEM), far, far] + [vmem] * len(got),
        out_specs=[vmem] * len(jobs),
        out_shape=[jax.ShapeDtypeStruct((rows, width), job[3]) for job in jobs],
        scratch_shapes=[
            pltpu.VMEM((rows, depth), BF),
            pltpu.VMEM((count, step, depth), BF),
            pltpu.SemaphoreType.DMA((count + 1,)),
        ],
        compiler_params=params(),
        cost_estimate=pl.CostEstimate(
            flops=count * rows * depth * width,
            bytes_accessed=count * width * depth,
            transcendentals=0,
        ),
        name="partial",
    )(where, attention, out_proj, *got)


def row_sums(value):
    rows, width = value.shape
    part = value[:, 0:128]
    for i in range(1, width // 128):
        part = part + value[:, i * 128 : (i + 1) * 128]
    return jnp.sum(part.T, axis=0, keepdims=True)


def hidden_kernel(own, sent, r1, r2, r3, residual, cot, gain, stats, hidden, sums):
    h = own[...] + sent[...].astype(F32) + residual[...].astype(F32)
    h = h + r1[...].astype(F32) + r2[...].astype(F32) + r3[...].astype(F32)
    hidden[...] = h
    scaled = cot[...].astype(F32) * gain[...].astype(F32)
    first = row_sums(h * h)
    second = row_sums(scaled * h)
    sums[...] = jnp.concatenate([first, second, stats[...], jnp.zeros((5, 128), F32)], axis=0)


def hidden_call(own, sent, r1, r2, r3, residual, cot, gain, stats):
    rows, width = own.shape
    big = pl.BlockSpec((128, width), lambda i: (i, 0))
    return pl.pallas_call(
        hidden_kernel,
        grid=(rows // 128,),
        in_specs=[big] * 7
        + [pl.BlockSpec((1, width), lambda i: (0, 0)), pl.BlockSpec((1, 128), lambda i: (0, 0))],
        out_specs=[big, pl.BlockSpec((8, 128), lambda i: (0, i))],
        out_shape=[
            jax.ShapeDtypeStruct((rows, width), F32),
            jax.ShapeDtypeStruct((8, rows), F32),
        ],
        compiler_params=params(),
        cost_estimate=pl.CostEstimate(
            flops=12 * rows * width, bytes_accessed=20 * rows * width, transcendentals=0
        ),
        name="hidden",
    )(own, sent, r1, r2, r3, residual, cot, gain, stats)


def column(row):
    return jnp.broadcast_to(row, (128, 128)).T


def spread(col, width):
    return jnp.concatenate([col] * (width // 128), axis=1)


def split_rows(value):
    high = value.astype(BF)
    rest = value - high.astype(F32)
    middle = rest.astype(BF)
    low = (rest - middle.astype(F32)).astype(BF)
    empty = jnp.zeros((EXTRA - 3, value.shape[1]), F32)
    parts = [high.astype(F32), middle.astype(F32), low.astype(F32), empty]
    return jnp.concatenate(parts, axis=0).astype(BF)


def joined(block):
    return jnp.sum(block.astype(F32), axis=0, keepdims=True)


def grad_kernel(
    features, tokens, hidden, cot, gain, s0, s1, s2, s3, info, grad, total
):
    i = pl.program_id(0)
    width = hidden.shape[1]
    sums = s0[...] + s1[...] + s2[...] + s3[...]
    square, inner = sums[0:1, :], sums[1:2, :]
    inverse = lax.rsqrt(square / features + 1e-06)
    reward, kept, group = info[0:1, :], info[1:2, :], info[2:3, :]

    def picked(offset):
        value = jnp.zeros_like(reward)
        for g in range(GROUPS):
            stat = jnp.broadcast_to(sums[2:3, offset + g : offset + g + 1], value.shape)
            value = jnp.where(group == float(g), stat, value)
        return value

    count = jnp.maximum(picked(0), 1.0)
    mean = picked(GROUPS) / count
    variance = picked(2 * GROUPS) / count - mean * mean
    advantage = (reward - mean) / jnp.sqrt(jnp.maximum(variance, 1.0))
    kept_tokens = jnp.broadcast_to(sums[2:3, 3 * GROUPS : 3 * GROUPS + 1], reward.shape)
    coef = -advantage * kept * tokens / jnp.maximum(kept_tokens, 1.0)
    first = coef * inverse
    second = coef * (inverse * inverse * inverse * inner / features)
    first = spread(column(first), width)
    second = spread(column(second), width)
    h = hidden[...]
    c = cot[...].astype(F32)
    grad[...] = (first * (c * gain[...].astype(F32)) - h * second).astype(BF)
    term = jnp.sum(first * c * h, axis=0, keepdims=True)
    @pl.when(i == 0)
    def _():
        total[...] = term

    @pl.when(i != 0)
    def _():
        total[...] += term


def grad_call(features, tokens, hidden, cot, gain, s0, s1, s2, s3, info):
    rows, width = hidden.shape
    big = pl.BlockSpec((128, width), lambda i: (i, 0))
    small = pl.BlockSpec((8, 128), lambda i: (0, i))
    return pl.pallas_call(
        functools.partial(grad_kernel, float(features), float(tokens)),
        grid=(rows // 128,),
        in_specs=[
            big,
            big,
            pl.BlockSpec((1, width), lambda i: (0, 0)),
        ]
        + [small] * 5,
        out_specs=[big, pl.BlockSpec((1, width), lambda i: (0, 0))],
        out_shape=[
            jax.ShapeDtypeStruct((rows, width), BF),
            jax.ShapeDtypeStruct((1, width), F32),
        ],
        compiler_params=params(),
        cost_estimate=pl.CostEstimate(
            flops=12 * rows * width, bytes_accessed=10 * rows * width, transcendentals=0
        ),
        name="grad",
    )(hidden, cot, gain, s0, s1, s2, s3, info)


def attention_kernel(where, *refs):
    pieces, w, out, buf, acc, sems = refs[:8], refs[8], refs[9], refs[10], refs[11], refs[12]
    x, c = where[2], where[3]
    step = buf.shape[1]
    copies = []
    for n in range(8):
        holder = (1 - c) if n % 2 else c
        piece = lax.rem(x + 4 - n // 2, 4) * 2 + holder
        row = pl.multiple_of(piece * step, step)
        copies.append(pltpu.make_async_copy(w.at[pl.ds(row, step)], buf.at[n], sems.at[n]))
        copies[-1].start()
    for n in range(8):
        copies[n].wait()
        term = jnp.dot(pieces[n][...], buf[n], preferred_element_type=F32)
        if n == 0:
            acc[...] = term
        elif n < 7:
            acc[...] += term
        else:
            out[...] = (acc[...] + term).astype(BF)


def attention_call(where, pieces, out_proj):
    rows, width = pieces[0].shape
    depth = out_proj.shape[1]
    vmem = pl.BlockSpec(memory_space=pltpu.VMEM)
    return pl.pallas_call(
        attention_kernel,
        in_specs=[pl.BlockSpec(memory_space=pltpu.SMEM)]
        + [vmem] * 8
        + [pl.BlockSpec(memory_space=pltpu.HBM)],
        out_specs=vmem,
        scratch_shapes=[
            pltpu.VMEM((8, width, depth), BF),
            pltpu.VMEM((rows, depth), F32),
            pltpu.SemaphoreType.DMA((8,)),
        ],
        out_shape=jax.ShapeDtypeStruct((rows, depth), BF),
        compiler_params=params(),
        cost_estimate=pl.CostEstimate(
            flops=2 * rows * depth * width * 8,
            bytes_accessed=2 * 8 * width * depth,
            transcendentals=0,
        ),
        name="attention_grad",
    )(where, *pieces, out_proj)


def first_pack_kernel(where, *refs):
    pieces, gain, outs = refs[:8], refs[8], refs[9:13]
    z, y, x, c = where[0], where[1], where[2], where[3]
    half = outs[0].shape[2]
    rows = outs[0].shape[1] - EXTRA
    for j in range(4):
        block = split_rows(gain[:, j * half : (j + 1) * half])
        for s in range(4):
            outs[s][j, rows : rows + EXTRA, :] = block
    for k in range(4):
        big_z = lax.rem(x + 4 - k, 4)
        for other in range(2):
            holder = (1 - c) if other else c
            for h in range(2):
                big_y = 2 * holder + h
                slot = jnp.where(c == 0, lax.rem(big_z + 4 - z, 4), lax.rem(big_y + 4 - y, 4))
                j = jnp.where(c == 0, big_y, big_z)
                start = pl.multiple_of(h * 2 * half + c * half, half)
                for s in range(4):

                    @pl.when(slot == s)
                    def _(s=s, j=j, start=start, piece=pieces[k * 2 + other]):
                        @pl.loop(0, rows // 64)
                        def _(r):
                            band = pl.ds(pl.multiple_of(r * 64, 64), 64)
                            outs[s][j, band, :] = piece[band, pl.ds(start, half)]


def second_pack_kernel(where, *refs):
    parts, outs = refs[:4], refs[4:8]
    rows = outs[0].shape[1] - EXTRA
    mine = jnp.where(where[3] == 0, where[1], where[0])
    tail = pl.ds(rows, EXTRA)
    for j in range(4):
        block = split_rows(sum(joined(part[j, tail, :]) for part in parts))
        for u in range(4):
            outs[u][j, tail, :] = block
    for u in range(4):
        j = lax.rem(mine + u, 4)
        for s in range(4):

            @pl.loop(0, rows // 64)
            def _(r, u=u, s=s, j=j):
                band = pl.ds(pl.multiple_of(r * 64, 64), 64)
                outs[u][s, band, :] = parts[s][j, band, :]


def pack_call(kernel, where, inputs, rows, half, name):
    vmem = pl.BlockSpec(memory_space=pltpu.VMEM)
    return pl.pallas_call(
        kernel,
        in_specs=[pl.BlockSpec(memory_space=pltpu.SMEM)] + [vmem] * len(inputs),
        out_specs=[vmem] * 4,
        out_shape=[jax.ShapeDtypeStruct((4, rows + EXTRA, half), BF)] * 4,
        compiler_params=pltpu.CompilerParams(vmem_limit_bytes=16 * 1024 * 1024),
        cost_estimate=pl.CostEstimate(
            flops=0, bytes_accessed=64 * rows * half, transcendentals=0
        ),
        name=name,
    )(where, *inputs)


def projection_kernel(members, first, last, where, gathered, *refs):
    count = len(members)
    mine, theirs = refs[:count], refs[count : 2 * count]
    refs = refs[2 * count :]
    before = None if first else refs[0]
    out = refs[0 if first else 1]
    z, y, c = where[0], where[1], where[3]
    half = out.shape[-2] // (2 if last else 1)
    rows = mine[0].shape[1] - EXTRA
    for n, parts in ((0, mine), (1, theirs)):
        z_first = (c == 0) if n == 0 else (c == 1)
        total = None if first else before[n]
        for m, u in enumerate(members):
            for s in range(4):
                dz, dy = jnp.where(z_first, s, u), jnp.where(z_first, u, s)
                row = lax.rem(z + 4 - dz, 4) * 4 + lax.rem(y + 4 - dy, 4)
                row = pl.multiple_of(row * rows, rows)
                term = lax.dot_general(
                    parts[m][s, 0:rows, :],
                    gathered[pl.ds(row, rows), :],
                    (((0,), (0,)), ((), ())),
                    preferred_element_type=F32,
                )
                total = term if total is None else total + term
        if last:
            holder = c if n == 0 else 1 - c
            start = pl.multiple_of(holder * half, half)
            out[pl.ds(start, half), :] = total.astype(BF)
        else:
            out[n] = total


def projection_call(where, mine, theirs, gathered, members, before, last):
    rows, half = mine[0].shape[1] - EXTRA, mine[0].shape[2]
    depth = gathered.shape[1]
    vmem = pl.BlockSpec(memory_space=pltpu.VMEM)
    blocks = 8 * len(members)
    picked = [mine[u] for u in members] + [theirs[u] for u in members]
    first = before is None
    return pl.pallas_call(
        functools.partial(projection_kernel, members, first, last),
        in_specs=[pl.BlockSpec(memory_space=pltpu.SMEM), vmem]
        + [vmem] * len(picked)
        + ([] if first else [vmem]),
        out_specs=vmem,
        out_shape=jax.ShapeDtypeStruct((2 * half, depth), BF)
        if last
        else jax.ShapeDtypeStruct((2, half, depth), F32),
        compiler_params=pltpu.CompilerParams(vmem_limit_bytes=24 * 1024 * 1024),
        cost_estimate=pl.CostEstimate(
            flops=2 * blocks * rows * half * depth,
            bytes_accessed=2 * blocks * rows * (depth + half),
            transcendentals=0,
        ),
        name="projection_grad",
    )(where, gathered, *picked, *([] if first else [before]))


def local_stats(rewards, group_ids, kept_flags, lengths):
    kept = kept_flags.astype(F32)
    onehot = (group_ids[None, :] == jnp.arange(GROUPS, dtype=jnp.int32)[:, None]).astype(F32)
    values = [
        jnp.sum(onehot * kept[None, :], axis=1),
        jnp.sum(onehot * (kept * rewards)[None, :], axis=1),
        jnp.sum(onehot * (kept * rewards * rewards)[None, :], axis=1),
        jnp.sum(kept * lengths[0].astype(F32))[None],
        jnp.zeros((128 - 3 * GROUPS - 1,), F32),
    ]
    return jnp.concatenate(values)[None, :]


def token_info(rewards, group_ids, kept_flags, lengths, rows):
    ends = jnp.cumsum(lengths[0])
    position = jnp.arange(rows, dtype=jnp.int32)
    segment = jnp.sum((position[None, :] >= ends[:, None]).astype(jnp.int32), axis=0)
    picks = (segment[None, :] == jnp.arange(rewards.shape[0], dtype=jnp.int32)[:, None]).astype(F32)
    values = [rewards, kept_flags.astype(F32), group_ids.astype(F32)]
    found = [jnp.sum(picks * value[:, None], axis=0, keepdims=True) for value in values]
    return jnp.concatenate(found + [jnp.zeros((5, rows), F32)], axis=0)


def shards(
    attention, residual, out_proj, norm_gain, cotangent, rewards, group_ids, kept_flags, lengths
):
    rows = attention.shape[0]
    features = out_proj.shape[0]
    d, t = lax.axis_index("dp"), lax.axis_index("tensor")
    where = jnp.stack([d // 4, d % 4, t // 2, t % 2]).astype(jnp.int32)
    gain = norm_gain[None, :]

    gathered = lax.all_gather(attention, "dp", axis=0, tiled=True)

    arrived = {}
    send2, keep2, send1, send3 = partial_products(
        where,
        attention,
        out_proj,
        [(2, True, False, BF), (2, False, False, F32), (1, True, False, BF), (3, True, False, BF)],
    )
    both = (keep2 + swap(send2).astype(F32)).astype(BF)
    arrived[2] = lax.ppermute(both, "tensor", x_shift(2))
    late_where, _ = lax.optimization_barrier((where, both))
    first, third, send0, keep0 = partial_products(
        late_where,
        attention,
        out_proj,
        [(1, False, True, BF), (3, False, True, BF), (0, True, False, BF), (0, False, False, F32)],
        [swap(send1), swap(send3)],
    )
    arrived[1] = lax.ppermute(first, "tensor", x_shift(1))
    arrived[3] = lax.ppermute(third, "tensor", x_shift(3))
    sent0 = swap(send0)
    stats = local_stats(rewards, group_ids, kept_flags, lengths)
    info = token_info(rewards, group_ids, kept_flags, lengths, rows)
    stats, info, arrived[2], _ = lax.optimization_barrier((stats, info, arrived[2], sent0))
    stats = sum(lax.ppermute(stats, ("dp", "tensor"), scattered(step)) for step in (0, 1))
    residual, info = lax.optimization_barrier((residual, info))
    hidden, sums = hidden_call(
        keep0, sent0, arrived[1], arrived[2], arrived[3], residual, cotangent, gain, stats
    )

    chip = sums + swap(sums)
    others = [lax.ppermute(chip, "tensor", x_shift(k)) for k in (1, 2, 3)]
    tokens = rows * lax.axis_size("dp")
    grad_residual, gain_term = grad_call(
        features, tokens, hidden, cotangent, gain, chip, *others, info
    )

    pieces = []
    for k in range(4):
        piece = grad_residual if k == 0 else lax.ppermute(grad_residual, "tensor", x_shift(k))
        pieces.extend([piece, swap(piece)])

    half = features // 32
    sends = pack_call(first_pack_kernel, where, pieces + [gain_term], rows, half, "first_pack")
    parts = [sends[0]] + [
        lax.ppermute(sends[k], ("dp", "tensor"), plane_shift(0, k)) for k in (1, 2, 3)
    ]
    late_where, _ = lax.optimization_barrier((where, sends))
    grad_attention = attention_call(late_where, pieces, out_proj)
    pack_where, _ = lax.optimization_barrier((where, grad_attention))
    sends = pack_call(second_pack_kernel, pack_where, parts, rows, half, "second_pack")
    mine = [sends[0]] + [
        lax.ppermute(sends[k], ("dp", "tensor"), plane_shift(1, k)) for k in (1, 2, 3)
    ]
    theirs = [swap(mine[0]), None, None, None]
    total = projection_call(where, mine, theirs, gathered, (0,), None, False)
    for k in (1, 3, 2):
        mine[k], total = lax.optimization_barrier((mine[k], total))
        theirs[k] = swap(mine[k])
    total = projection_call(where, mine, theirs, gathered, (1, 3, 2), total, True)
    tails = [part[:, rows:, :].astype(F32) for part in mine]
    grad_gain = jnp.sum(sum(tails), axis=1).reshape(-1)
    return (grad_attention, total, grad_residual, grad_gain)


def solution(mesh):
    return jax.shard_map(
        shards,
        mesh=mesh,
        in_specs=(
            P("dp", "tensor"),
            P("dp", "tensor"),
            P(None, "tensor"),
            P("tensor"),
            P("dp", "tensor"),
            P("dp"),
            P("dp"),
            P("dp"),
            P("dp", None),
        ),
        out_specs=(P("dp", "tensor"), P("dp", "tensor"), P("dp", "tensor"), P("tensor")),
        check_vma=False,
    )
```

```python
import functools

import jax
import jax.numpy as jnp
from jax import lax
from jax.experimental import pallas as pl
from jax.experimental.pallas import tpu as pltpu
from jax.sharding import PartitionSpec as P

BF = jnp.bfloat16
F32 = jnp.float32
LIMIT = 48 * 1024 * 1024
SMALL = 16 * 1024 * 1024
EXTRA = 16
GROUPS = 4
CORE_SWAP = [(t, t ^ 1) for t in range(8)]


def x_shift(k):
    return [(t, ((t // 2 + k) % 4) * 2 + t % 2) for t in range(8)]


def plane_shift(stage, k):
    pairs = []
    for d in range(16):
        for t in range(8):
            z, y = d // 4, d % 4
            if (t % 2) == stage:
                z = (z + k) % 4
            else:
                y = (y + k) % 4
            pairs.append((d * 8 + t, (z * 4 + y) * 8 + t))
    return pairs


def scattered(step):
    return [(d * 8 + t, ((d + 2 * t + step) % 16) * 8 + t) for d in range(16) for t in range(8)]


def swap(value):
    return lax.ppermute(value, "tensor", CORE_SWAP)


def params():
    return pltpu.CompilerParams(vmem_limit_bytes=LIMIT)


def partial_kernel(jobs, where, att, w, *refs):
    ins = sum(1 for job in jobs if job[2])
    got, outs = refs[:ins], refs[ins:-2]
    buf, sems = refs[-2:]
    x, c = where[2], where[3]
    step = buf.shape[1]
    copies = []
    for shift, other, _, _ in jobs:
        piece = lax.rem(x + shift, 4) * 2 + (1 - c if other else c)
        for h in range(2):
            row = pl.multiple_of((piece * 2 + h) * step, step)
            n = len(copies)
            copies.append(pltpu.make_async_copy(w.at[pl.ds(row, step)], buf.at[n], sems.at[n]))
    for copy in copies:
        copy.start()
    used = 0
    for n, (_, _, add, _) in enumerate(jobs):
        if add:
            used += 1

        for h in range(2):
            copies[2 * n + h].wait()

        @pl.loop(0, 2)
        def _(h, n=n, add=add, used=used):
            columns = pl.ds(pl.multiple_of(h * step, step), step)
            term = lax.dot_general(
                att[...], buf[2 * n + h], (((1,), (1,)), ((), ())), preferred_element_type=F32
            )
            if add:
                term += got[used - 1][:, columns].astype(F32)
            outs[n][:, columns] = term.astype(outs[n].dtype)


def partial_products(where, attention, out_proj, jobs, got=()):
    rows, depth = attention.shape
    width = out_proj.shape[0] // 8
    step = width // 2
    count = 2 * len(jobs)
    vmem = pl.BlockSpec(memory_space=pltpu.VMEM)
    far = pl.BlockSpec(memory_space=pltpu.HBM)
    return pl.pallas_call(
        functools.partial(partial_kernel, jobs),
        in_specs=[pl.BlockSpec(memory_space=pltpu.SMEM), vmem, far] + [vmem] * len(got),
        out_specs=[vmem] * len(jobs),
        out_shape=[jax.ShapeDtypeStruct((rows, width), job[3]) for job in jobs],
        scratch_shapes=[
            pltpu.VMEM((count, step, depth), BF),
            pltpu.SemaphoreType.DMA((count,)),
        ],
        compiler_params=params(),
        cost_estimate=pl.CostEstimate(
            flops=count * rows * depth * width,
            bytes_accessed=count * width * depth,
            transcendentals=0,
        ),
        name="partial",
    )(where, attention, out_proj, *got)


def row_sums(value):
    rows, width = value.shape
    part = value[:, 0:128]
    for i in range(1, width // 128):
        part = part + value[:, i * 128 : (i + 1) * 128]
    return jnp.sum(part.T, axis=0, keepdims=True)


def hidden_kernel(own, r1, r2, r3, residual, cot, gain, stats, hidden, sums):
    @pl.loop(0, own.shape[0] // 128)
    def _(i):
        band = pl.ds(pl.multiple_of(i * 128, 128), 128)
        h = own[band, :] + residual[band, :].astype(F32)
        h = h + r1[band, :].astype(F32) + r2[band, :].astype(F32) + r3[band, :].astype(F32)
        hidden[band, :] = h
        scaled = cot[band, :].astype(F32) * gain[...].astype(F32)
        first = row_sums(h * h)
        second = row_sums(scaled * h)
        rest = [stats[...], jnp.zeros((5, 128), F32)]
        sums[:, band] = jnp.concatenate([first, second] + rest, axis=0)


def hidden_call(own, r1, r2, r3, residual, cot, gain, stats):
    rows, width = own.shape
    vmem = pl.BlockSpec(memory_space=pltpu.VMEM)
    return pl.pallas_call(
        hidden_kernel,
        in_specs=[vmem] * 8,
        out_specs=[vmem] * 2,
        out_shape=[
            jax.ShapeDtypeStruct((rows, width), F32),
            jax.ShapeDtypeStruct((8, rows), F32),
        ],
        compiler_params=pltpu.CompilerParams(vmem_limit_bytes=SMALL),
        cost_estimate=pl.CostEstimate(
            flops=12 * rows * width, bytes_accessed=20 * rows * width, transcendentals=0
        ),
        name="hidden",
    )(own, r1, r2, r3, residual, cot, gain, stats)


def column(row):
    return jnp.broadcast_to(row, (128, 128)).T


def spread(col, width):
    return jnp.concatenate([col] * (width // 128), axis=1)


def split_rows(value):
    high = value.astype(BF)
    rest = value - high.astype(F32)
    middle = rest.astype(BF)
    low = (rest - middle.astype(F32)).astype(BF)
    empty = jnp.zeros((EXTRA - 3, value.shape[1]), F32)
    parts = [high.astype(F32), middle.astype(F32), low.astype(F32), empty]
    return jnp.concatenate(parts, axis=0).astype(BF)


def joined(block):
    return jnp.sum(block.astype(F32), axis=0, keepdims=True)


def grad_kernel(features, tokens, hidden, cot, gain, s0, s1, s2, s3, info, grad, piece, total):
    width = hidden.shape[1]
    total[...] = jnp.zeros_like(total)

    @pl.loop(0, hidden.shape[0] // 128)
    def _(i):
        band = pl.ds(pl.multiple_of(i * 128, 128), 128)
        sums = s0[:, band] + s1[:, band] + s2[:, band] + s3[:, band]
        square, inner = sums[0:1, :], sums[1:2, :]
        inverse = lax.rsqrt(square / features + 1e-06)
        reward, kept, group = info[0:1, band], info[1:2, band], info[2:3, band]

        def picked(offset):
            value = jnp.zeros_like(reward)
            for g in range(GROUPS):
                stat = jnp.broadcast_to(sums[2:3, offset + g : offset + g + 1], value.shape)
                value = jnp.where(group == float(g), stat, value)
            return value

        count = jnp.maximum(picked(0), 1.0)
        mean = picked(GROUPS) / count
        variance = picked(2 * GROUPS) / count - mean * mean
        advantage = (reward - mean) / jnp.sqrt(jnp.maximum(variance, 1.0))
        kept_tokens = jnp.broadcast_to(sums[2:3, 3 * GROUPS : 3 * GROUPS + 1], reward.shape)
        coef = -advantage * kept * tokens / jnp.maximum(kept_tokens, 1.0)
        first = spread(column(coef * inverse), width)
        second = spread(column(coef * (inverse * inverse * inverse * inner / features)), width)
        h = hidden[band, :]
        c = cot[band, :].astype(F32)
        value = (first * (c * gain[...].astype(F32)) - h * second).astype(BF)
        grad[band, :] = value
        piece[band, :] = value
        total[...] += jnp.sum(first * c * h, axis=0, keepdims=True)


def grad_call(features, tokens, hidden, cot, gain, s0, s1, s2, s3, info):
    rows, width = hidden.shape
    vmem = pl.BlockSpec(memory_space=pltpu.VMEM)
    return pl.pallas_call(
        functools.partial(grad_kernel, float(features), float(tokens)),
        in_specs=[vmem] * 8,
        out_specs=[vmem] * 3,
        out_shape=[
            jax.ShapeDtypeStruct((rows, width), BF),
            jax.ShapeDtypeStruct((rows, width), BF),
            jax.ShapeDtypeStruct((1, width), F32),
        ],
        compiler_params=pltpu.CompilerParams(vmem_limit_bytes=SMALL),
        cost_estimate=pl.CostEstimate(
            flops=12 * rows * width, bytes_accessed=8 * rows * width, transcendentals=0
        ),
        name="grad",
    )(hidden, cot, gain, s0, s1, s2, s3, info)


def attention_kernel(where, *refs):
    pieces, w, out, buf, acc, sems = refs[:8], refs[8], refs[9], refs[10], refs[11], refs[12]
    x, c = where[2], where[3]
    step = buf.shape[1]
    copies = []
    for n in range(8):
        holder = (1 - c) if n % 2 else c
        piece = lax.rem(x + 4 - n // 2, 4) * 2 + holder
        row = pl.multiple_of(piece * step, step)
        copies.append(pltpu.make_async_copy(w.at[pl.ds(row, step)], buf.at[n], sems.at[n]))
        copies[-1].start()
    for n in range(8):
        copies[n].wait()
        term = jnp.dot(pieces[n][...], buf[n], preferred_element_type=F32)
        if n == 0:
            acc[...] = term
        elif n < 7:
            acc[...] += term
        else:
            out[...] = (acc[...] + term).astype(BF)


def attention_call(where, pieces, out_proj):
    rows, width = pieces[0].shape
    depth = out_proj.shape[1]
    vmem = pl.BlockSpec(memory_space=pltpu.VMEM)
    return pl.pallas_call(
        attention_kernel,
        in_specs=[pl.BlockSpec(memory_space=pltpu.SMEM)]
        + [vmem] * 8
        + [pl.BlockSpec(memory_space=pltpu.HBM)],
        out_specs=vmem,
        scratch_shapes=[
            pltpu.VMEM((8, width, depth), BF),
            pltpu.VMEM((rows, depth), F32),
            pltpu.SemaphoreType.DMA((8,)),
        ],
        out_shape=jax.ShapeDtypeStruct((rows, depth), BF),
        compiler_params=params(),
        cost_estimate=pl.CostEstimate(
            flops=2 * rows * depth * width * 8,
            bytes_accessed=2 * 8 * width * depth,
            transcendentals=0,
        ),
        name="attention_grad",
    )(where, *pieces, out_proj)


def first_pack_kernel(where, *refs):
    pieces, gain, outs = refs[:8], refs[8], refs[9:13]
    z, y, x, c = where[0], where[1], where[2], where[3]
    half = outs[0].shape[2]
    rows = outs[0].shape[1] - EXTRA
    for j in range(4):
        block = split_rows(gain[:, j * half : (j + 1) * half])
        for s in range(4):
            outs[s][j, rows : rows + EXTRA, :] = block
    for k in range(4):
        big_z = lax.rem(x + 4 - k, 4)
        for other in range(2):
            holder = (1 - c) if other else c
            for h in range(2):
                big_y = 2 * holder + h
                slot = jnp.where(c == 0, lax.rem(big_z + 4 - z, 4), lax.rem(big_y + 4 - y, 4))
                j = jnp.where(c == 0, big_y, big_z)
                start = pl.multiple_of(h * 2 * half + c * half, half)
                for s in range(4):

                    @pl.when(slot == s)
                    def _(s=s, j=j, start=start, piece=pieces[k * 2 + other]):
                        @pl.loop(0, rows // 128)
                        def _(r):
                            band = pl.ds(pl.multiple_of(r * 128, 128), 128)
                            outs[s][j, band, :] = piece[band, pl.ds(start, half)]


def second_pack_kernel(where, *refs):
    parts, outs = refs[:4], refs[4:8]
    rows = outs[0].shape[1] - EXTRA
    mine = jnp.where(where[3] == 0, where[1], where[0])
    tail = pl.ds(rows, EXTRA)
    for j in range(4):
        block = split_rows(sum(joined(part[j, tail, :]) for part in parts))
        for u in range(4):
            outs[u][j, tail, :] = block
    for u in range(4):
        j = lax.rem(mine + u, 4)
        for s in range(4):
            outs[u][s, 0:rows, :] = parts[s][j, 0:rows, :]


def pack_call(kernel, where, inputs, rows, half, name):
    vmem = pl.BlockSpec(memory_space=pltpu.VMEM)
    return pl.pallas_call(
        kernel,
        in_specs=[pl.BlockSpec(memory_space=pltpu.SMEM)] + [vmem] * len(inputs),
        out_specs=[vmem] * 4,
        out_shape=[jax.ShapeDtypeStruct((4, rows + EXTRA, half), BF)] * 4,
        compiler_params=pltpu.CompilerParams(vmem_limit_bytes=16 * 1024 * 1024),
        cost_estimate=pl.CostEstimate(
            flops=0, bytes_accessed=64 * rows * half, transcendentals=0
        ),
        name=name,
    )(where, *inputs)


def projection_kernel(members, first, last, where, gathered, *refs):
    count = sum(len(group) for group in members)
    parts = refs[:count]
    refs = refs[count:]
    before = None if first else refs[0]
    out = refs[2 if last else 0 if first else 1]
    if last:
        refs[3][...] = jnp.sum(refs[1][...], axis=0, keepdims=True)
    z, y, c = where[0], where[1], where[3]
    half = out.shape[-2] // (2 if last else 1)
    rows = parts[0].shape[1] - EXTRA
    used = 0
    for n in range(2):
        z_first = (c == 0) if n == 0 else (c == 1)
        total = None if first else before[n]
        for u in members[n]:
            part = parts[used]
            used += 1
            for s in range(4):
                dz, dy = jnp.where(z_first, s, u), jnp.where(z_first, u, s)
                row = lax.rem(z + 4 - dz, 4) * 4 + lax.rem(y + 4 - dy, 4)
                row = pl.multiple_of(row * rows, rows)
                term = lax.dot_general(
                    part[s, 0:rows, :],
                    gathered[pl.ds(row, rows), :],
                    (((0,), (0,)), ((), ())),
                    preferred_element_type=F32,
                )
                total = term if total is None else total + term
        if last:
            holder = c if n == 0 else 1 - c
            start = pl.multiple_of(holder * half, half)
            out[pl.ds(start, half), :] = total.astype(BF)
        else:
            out[n] = total


def projection_call(where, mine, theirs, gathered, members, before, tails=None):
    rows, half = mine[0].shape[1] - EXTRA, mine[0].shape[2]
    depth = gathered.shape[1]
    vmem = pl.BlockSpec(memory_space=pltpu.VMEM)
    picked = [mine[u] for u in members[0]] + [theirs[u] for u in members[1]]
    blocks = 4 * len(picked)
    first, last = before is None, tails is not None
    return pl.pallas_call(
        functools.partial(projection_kernel, members, first, last),
        in_specs=[pl.BlockSpec(memory_space=pltpu.SMEM), vmem]
        + [vmem] * len(picked)
        + ([] if first else [vmem])
        + ([vmem] if last else []),
        out_specs=[vmem, vmem] if last else vmem,
        out_shape=[
            jax.ShapeDtypeStruct((2 * half, depth), BF),
            jax.ShapeDtypeStruct((1, 4 * half), F32),
        ]
        if last
        else jax.ShapeDtypeStruct((2, half, depth), F32),
        compiler_params=pltpu.CompilerParams(vmem_limit_bytes=24 * 1024 * 1024),
        cost_estimate=pl.CostEstimate(
            flops=2 * blocks * rows * half * depth,
            bytes_accessed=2 * blocks * rows * (depth + half),
            transcendentals=0,
        ),
        name="projection_grad",
    )(where, gathered, *picked, *([] if first else [before]), *([tails] if last else []))


def local_stats(rewards, group_ids, kept_flags, lengths):
    kept = kept_flags.astype(F32)
    onehot = (group_ids[None, :] == jnp.arange(GROUPS, dtype=jnp.int32)[:, None]).astype(F32)
    values = [
        jnp.sum(onehot * kept[None, :], axis=1),
        jnp.sum(onehot * (kept * rewards)[None, :], axis=1),
        jnp.sum(onehot * (kept * rewards * rewards)[None, :], axis=1),
        jnp.sum(kept * lengths[0].astype(F32))[None],
        jnp.zeros((128 - 3 * GROUPS - 1,), F32),
    ]
    return jnp.concatenate(values)[None, :]


def token_info(rewards, group_ids, kept_flags, lengths, rows):
    ends = jnp.cumsum(lengths[0])
    position = jnp.arange(rows, dtype=jnp.int32)
    segment = jnp.sum((position[None, :] >= ends[:, None]).astype(jnp.int32), axis=0)
    picks = (segment[None, :] == jnp.arange(rewards.shape[0], dtype=jnp.int32)[:, None]).astype(F32)
    values = [rewards, kept_flags.astype(F32), group_ids.astype(F32)]
    found = [jnp.sum(picks * value[:, None], axis=0, keepdims=True) for value in values]
    return jnp.concatenate(found + [jnp.zeros((5, rows), F32)], axis=0)


def shards(
    attention, residual, out_proj, norm_gain, cotangent, rewards, group_ids, kept_flags, lengths
):
    rows = attention.shape[0]
    features = out_proj.shape[0]
    d, t = lax.axis_index("dp"), lax.axis_index("tensor")
    where = jnp.stack([d // 4, d % 4, t // 2, t % 2]).astype(jnp.int32)
    gain = norm_gain[None, :]

    gathered = lax.all_gather(attention, "dp", axis=0, tiled=True)

    arrived = {}
    send2, keep2, send1, send3 = partial_products(
        where,
        attention,
        out_proj,
        [(2, True, False, BF), (2, False, False, F32), (1, True, False, BF), (3, True, False, BF)],
    )
    both = (keep2 + swap(send2).astype(F32)).astype(BF)
    arrived[2] = lax.ppermute(both, "tensor", x_shift(2))
    late_where, _ = lax.optimization_barrier((where, both))
    first, third, send0 = partial_products(
        late_where,
        attention,
        out_proj,
        [(1, False, True, BF), (3, False, True, BF), (0, True, False, BF)],
        [swap(send1), swap(send3)],
    )
    arrived[1] = lax.ppermute(first, "tensor", x_shift(1))
    arrived[3] = lax.ppermute(third, "tensor", x_shift(3))
    stats = local_stats(rewards, group_ids, kept_flags, lengths)
    info = token_info(rewards, group_ids, kept_flags, lengths, rows)
    stats, info, _ = lax.optimization_barrier((stats, info, third))
    late_where, arrived[2] = lax.optimization_barrier((where, arrived[2]))
    stats = sum(lax.ppermute(stats, ("dp", "tensor"), scattered(step)) for step in (0, 1))
    (own,) = partial_products(
        late_where, attention, out_proj, [(0, False, True, F32)], [swap(send0)]
    )
    residual, info = lax.optimization_barrier((residual, info))
    hidden, sums = hidden_call(
        own, arrived[1], arrived[2], arrived[3], residual, cotangent, gain, stats
    )

    chip = sums + swap(sums)
    others = [lax.ppermute(chip, "tensor", x_shift(k)) for k in (1, 2, 3)]
    tokens = rows * lax.axis_size("dp")
    grad_residual, own_piece, gain_term = grad_call(
        features, tokens, hidden, cotangent, gain, chip, *others, info
    )

    pieces = []
    for k in range(4):
        piece = own_piece if k == 0 else lax.ppermute(own_piece, "tensor", x_shift(k))
        pieces.extend([piece, swap(piece)])

    half = features // 32
    sends = pack_call(first_pack_kernel, where, pieces + [gain_term], rows, half, "first_pack")
    parts = [sends[0]] + [
        lax.ppermute(sends[k], ("dp", "tensor"), plane_shift(0, k)) for k in (1, 2, 3)
    ]
    late_where, _ = lax.optimization_barrier((where, sends))
    grad_attention = attention_call(late_where, pieces, out_proj)
    pack_where, _ = lax.optimization_barrier((where, grad_attention))
    sends = pack_call(second_pack_kernel, pack_where, parts, rows, half, "second_pack")
    mine = [sends[0]] + [
        lax.ppermute(sends[k], ("dp", "tensor"), plane_shift(1, k)) for k in (1, 2, 3)
    ]
    theirs = [swap(mine[0]), None, None, None]
    total = projection_call(where, mine, theirs, gathered, ((0,), (0,)), None)
    for k in (1, 3, 2):
        mine[k], total = lax.optimization_barrier((mine[k], total))
        theirs[k] = swap(mine[k])
    total = projection_call(where, mine, theirs, gathered, ((1, 3, 2), ()), total)
    tails = sum(part[:, rows:, :].astype(F32) for part in mine)
    tails = jnp.concatenate([tails[j] for j in range(4)], axis=1)
    grad_out_proj, grad_gain = projection_call(
        where, mine, theirs, gathered, ((), (1, 3, 2)), total, tails
    )
    return (grad_attention, grad_out_proj, grad_residual, grad_gain[0])


def solution(mesh):
    return jax.shard_map(
        shards,
        mesh=mesh,
        in_specs=(
            P("dp", "tensor"),
            P("dp", "tensor"),
            P(None, "tensor"),
            P("tensor"),
            P("dp", "tensor"),
            P("dp"),
            P("dp"),
            P("dp"),
            P("dp", None),
        ),
        out_specs=(P("dp", "tensor"), P("dp", "tensor"), P("dp", "tensor"), P("tensor")),
        check_vma=False,
    )
```

```python
import functools

import jax
import jax.numpy as jnp
from jax import lax
from jax.experimental import pallas as pl
from jax.experimental.pallas import tpu as pltpu
from jax.sharding import PartitionSpec as P

BF = jnp.bfloat16
F32 = jnp.float32
LIMIT = 48 * 1024 * 1024
SMALL = 16 * 1024 * 1024
EXTRA = 16
GROUPS = 4
CORE_SWAP = [(t, t ^ 1) for t in range(8)]


def x_shift(k):
    return [(t, ((t // 2 + k) % 4) * 2 + t % 2) for t in range(8)]


def plane_shift(stage, k):
    pairs = []
    for d in range(16):
        for t in range(8):
            z, y = d // 4, d % 4
            if (t % 2) == stage:
                z = (z + k) % 4
            else:
                y = (y + k) % 4
            pairs.append((d * 8 + t, (z * 4 + y) * 8 + t))
    return pairs


def scattered(step):
    return [(d * 8 + t, ((d + 2 * t + step) % 16) * 8 + t) for d in range(16) for t in range(8)]


def swap(value):
    return lax.ppermute(value, "tensor", CORE_SWAP)


def params():
    return pltpu.CompilerParams(vmem_limit_bytes=LIMIT)


def partial_kernel(jobs, where, att, w, *refs):
    ins = sum(1 for job in jobs if job[2])
    got, outs = refs[:ins], refs[ins:-2]
    buf, sems = refs[-2:]
    x, c = where[2], where[3]
    step = buf.shape[1]
    copies = []
    for shift, other, _, _ in jobs:
        piece = lax.rem(x + shift, 4) * 2 + (1 - c if other else c)
        for h in range(2):
            row = pl.multiple_of((piece * 2 + h) * step, step)
            n = len(copies)
            copies.append(pltpu.make_async_copy(w.at[pl.ds(row, step)], buf.at[n], sems.at[n]))
    for copy in copies:
        copy.start()
    used = 0
    for n, (_, _, add, _) in enumerate(jobs):
        if add:
            used += 1

        for h in range(2):
            copies[2 * n + h].wait()

        @pl.loop(0, 2)
        def _(h, n=n, add=add, used=used):
            columns = pl.ds(pl.multiple_of(h * step, step), step)
            term = lax.dot_general(
                att[...], buf[2 * n + h], (((1,), (1,)), ((), ())), preferred_element_type=F32
            )
            if add:
                term += got[used - 1][:, columns].astype(F32)
            outs[n][:, columns] = term.astype(outs[n].dtype)


def partial_products(where, attention, out_proj, jobs, got=()):
    rows, depth = attention.shape
    width = out_proj.shape[0] // 8
    step = width // 2
    count = 2 * len(jobs)
    vmem = pl.BlockSpec(memory_space=pltpu.VMEM)
    far = pl.BlockSpec(memory_space=pltpu.HBM)
    return pl.pallas_call(
        functools.partial(partial_kernel, jobs),
        in_specs=[pl.BlockSpec(memory_space=pltpu.SMEM), vmem, far] + [vmem] * len(got),
        out_specs=[vmem] * len(jobs),
        out_shape=[jax.ShapeDtypeStruct((rows, width), job[3]) for job in jobs],
        scratch_shapes=[
            pltpu.VMEM((count, step, depth), BF),
            pltpu.SemaphoreType.DMA((count,)),
        ],
        compiler_params=params(),
        cost_estimate=pl.CostEstimate(
            flops=count * rows * depth * width,
            bytes_accessed=count * width * depth,
            transcendentals=0,
        ),
        name="partial",
    )(where, attention, out_proj, *got)


def halves_kernel(first, second, top, bottom):
    rows = top.shape[0]

    @pl.loop(0, rows // 64)
    def _(i):
        for n, out in ((0, top), (1, bottom)):
            band = pl.ds(pl.multiple_of(n * rows + i * 64, 64), 64)
            here = pl.ds(pl.multiple_of(i * 64, 64), 64)
            out[here, :] = (first[band, :] + second[band, :].astype(F32)).astype(BF)


def passed_kernel(first, third, top, bottom, next_first, next_third):
    rows = top.shape[0]

    @pl.loop(0, rows // 64)
    def _(i):
        low = pl.ds(pl.multiple_of(i * 64, 64), 64)
        high = pl.ds(pl.multiple_of(rows + i * 64, 64), 64)
        next_first[low, :] = (first[low, :] + top[low, :].astype(F32)).astype(BF)
        next_first[high, :] = first[high, :].astype(BF)
        next_third[low, :] = third[low, :].astype(BF)
        next_third[high, :] = (third[high, :] + bottom[low, :].astype(F32)).astype(BF)


def joined_kernel(top, bottom, out):
    rows = top.shape[0]

    @pl.loop(0, rows // 64)
    def _(i):
        low = pl.ds(pl.multiple_of(i * 64, 64), 64)
        high = pl.ds(pl.multiple_of(rows + i * 64, 64), 64)
        out[low, :] = top[low, :]
        out[high, :] = bottom[low, :]


def small_call(kernel, inputs, shapes, name):
    vmem = pl.BlockSpec(memory_space=pltpu.VMEM)
    return pl.pallas_call(
        kernel,
        in_specs=[vmem] * len(inputs),
        out_specs=[vmem] * len(shapes),
        out_shape=[jax.ShapeDtypeStruct(shape, BF) for shape in shapes],
        compiler_params=pltpu.CompilerParams(vmem_limit_bytes=SMALL),
        cost_estimate=pl.CostEstimate(
            flops=inputs[0].size, bytes_accessed=8 * inputs[0].size, transcendentals=0
        ),
        name=name,
    )(*inputs)


def row_sums(value):
    rows, width = value.shape
    part = value[:, 0:128]
    for i in range(1, width // 128):
        part = part + value[:, i * 128 : (i + 1) * 128]
    return jnp.sum(part.T, axis=0, keepdims=True)


def hidden_kernel(own, r1, r3, residual, cot, gain, even, odd, hidden, sums):
    @pl.loop(0, own.shape[0] // 128)
    def _(i):
        band = pl.ds(pl.multiple_of(i * 128, 128), 128)
        h = own[band, :] + residual[band, :].astype(F32)
        h = h + r1[band, :].astype(F32) + r3[band, :].astype(F32)
        hidden[band, :] = h
        scaled = cot[band, :].astype(F32) * gain[...].astype(F32)
        first = row_sums(h * h)
        second = row_sums(scaled * h)
        rest = [even[...] + odd[...], jnp.zeros((5, 128), F32)]
        sums[:, band] = jnp.concatenate([first, second] + rest, axis=0)


def hidden_call(own, r1, r3, residual, cot, gain, even, odd):
    rows, width = own.shape
    vmem = pl.BlockSpec(memory_space=pltpu.VMEM)
    return pl.pallas_call(
        hidden_kernel,
        in_specs=[vmem] * 8,
        out_specs=[vmem] * 2,
        out_shape=[
            jax.ShapeDtypeStruct((rows, width), F32),
            jax.ShapeDtypeStruct((8, rows), F32),
        ],
        compiler_params=pltpu.CompilerParams(vmem_limit_bytes=SMALL),
        cost_estimate=pl.CostEstimate(
            flops=12 * rows * width, bytes_accessed=20 * rows * width, transcendentals=0
        ),
        name="hidden",
    )(own, r1, r3, residual, cot, gain, even, odd)


def column(row):
    return jnp.broadcast_to(row, (128, 128)).T


def spread(col, width):
    return jnp.concatenate([col] * (width // 128), axis=1)


def split_rows(value):
    high = value.astype(BF)
    rest = value - high.astype(F32)
    middle = rest.astype(BF)
    low = (rest - middle.astype(F32)).astype(BF)
    empty = jnp.zeros((EXTRA - 3, value.shape[1]), F32)
    parts = [high.astype(F32), middle.astype(F32), low.astype(F32), empty]
    return jnp.concatenate(parts, axis=0).astype(BF)


def joined(block):
    return jnp.sum(block.astype(F32), axis=0, keepdims=True)


def grad_kernel(features, tokens, hidden, cot, gain, s0, s1, s2, s3, info, grad, piece, total):
    width = hidden.shape[1]
    total[...] = jnp.zeros_like(total)

    @pl.loop(0, hidden.shape[0] // 128)
    def _(i):
        band = pl.ds(pl.multiple_of(i * 128, 128), 128)
        sums = s0[:, band] + s1[:, band] + s2[:, band] + s3[:, band]
        square, inner = sums[0:1, :], sums[1:2, :]
        inverse = lax.rsqrt(square / features + 1e-06)
        reward, kept, group = info[0:1, band], info[1:2, band], info[2:3, band]

        def picked(offset):
            value = jnp.zeros_like(reward)
            for g in range(GROUPS):
                stat = jnp.broadcast_to(sums[2:3, offset + g : offset + g + 1], value.shape)
                value = jnp.where(group == float(g), stat, value)
            return value

        count = jnp.maximum(picked(0), 1.0)
        mean = picked(GROUPS) / count
        variance = picked(2 * GROUPS) / count - mean * mean
        advantage = (reward - mean) / jnp.sqrt(jnp.maximum(variance, 1.0))
        kept_tokens = jnp.broadcast_to(sums[2:3, 3 * GROUPS : 3 * GROUPS + 1], reward.shape)
        coef = -advantage * kept * tokens / jnp.maximum(kept_tokens, 1.0)
        first = spread(column(coef * inverse), width)
        second = spread(column(coef * (inverse * inverse * inverse * inner / features)), width)
        h = hidden[band, :]
        c = cot[band, :].astype(F32)
        value = (first * (c * gain[...].astype(F32)) - h * second).astype(BF)
        grad[band, :] = value
        piece[band, :] = value
        total[...] += jnp.sum(first * c * h, axis=0, keepdims=True)


def grad_call(features, tokens, hidden, cot, gain, s0, s1, s2, s3, info):
    rows, width = hidden.shape
    vmem = pl.BlockSpec(memory_space=pltpu.VMEM)
    return pl.pallas_call(
        functools.partial(grad_kernel, float(features), float(tokens)),
        in_specs=[vmem] * 8,
        out_specs=[vmem] * 3,
        out_shape=[
            jax.ShapeDtypeStruct((rows, width), BF),
            jax.ShapeDtypeStruct((rows, width), BF),
            jax.ShapeDtypeStruct((1, width), F32),
        ],
        compiler_params=pltpu.CompilerParams(vmem_limit_bytes=SMALL),
        cost_estimate=pl.CostEstimate(
            flops=12 * rows * width, bytes_accessed=8 * rows * width, transcendentals=0
        ),
        name="grad",
    )(hidden, cot, gain, s0, s1, s2, s3, info)


def attention_kernel(where, *refs):
    pieces, w, out, buf, acc, sems = refs[:8], refs[8], refs[9], refs[10], refs[11], refs[12]
    x, c = where[2], where[3]
    step = buf.shape[1]
    copies = []
    for n in range(8):
        holder = (1 - c) if n % 2 else c
        piece = lax.rem(x + 4 - n // 2, 4) * 2 + holder
        row = pl.multiple_of(piece * step, step)
        copies.append(pltpu.make_async_copy(w.at[pl.ds(row, step)], buf.at[n], sems.at[n]))
        copies[-1].start()
    for n in range(8):
        copies[n].wait()
        term = jnp.dot(pieces[n][...], buf[n], preferred_element_type=F32)
        if n == 0:
            acc[...] = term
        elif n < 7:
            acc[...] += term
        else:
            out[...] = (acc[...] + term).astype(BF)


def attention_call(where, pieces, out_proj):
    rows, width = pieces[0].shape
    depth = out_proj.shape[1]
    vmem = pl.BlockSpec(memory_space=pltpu.VMEM)
    return pl.pallas_call(
        attention_kernel,
        in_specs=[pl.BlockSpec(memory_space=pltpu.SMEM)]
        + [vmem] * 8
        + [pl.BlockSpec(memory_space=pltpu.HBM)],
        out_specs=vmem,
        scratch_shapes=[
            pltpu.VMEM((8, width, depth), BF),
            pltpu.VMEM((rows, depth), F32),
            pltpu.SemaphoreType.DMA((8,)),
        ],
        out_shape=jax.ShapeDtypeStruct((rows, depth), BF),
        compiler_params=params(),
        cost_estimate=pl.CostEstimate(
            flops=2 * rows * depth * width * 8,
            bytes_accessed=2 * 8 * width * depth,
            transcendentals=0,
        ),
        name="attention_grad",
    )(where, *pieces, out_proj)


def first_pack_kernel(where, *refs):
    pieces, gain, outs = refs[:8], refs[8], refs[9:13]
    z, y, x, c = where[0], where[1], where[2], where[3]
    half = outs[0].shape[2]
    rows = outs[0].shape[1] - EXTRA
    for j in range(4):
        block = split_rows(gain[:, j * half : (j + 1) * half])
        for s in range(4):
            outs[s][j, rows : rows + EXTRA, :] = block
    for k in range(4):
        big_z = lax.rem(x + 4 - k, 4)
        for other in range(2):
            holder = (1 - c) if other else c
            for h in range(2):
                big_y = 2 * holder + h
                slot = jnp.where(c == 0, lax.rem(big_z + 4 - z, 4), lax.rem(big_y + 4 - y, 4))
                j = jnp.where(c == 0, big_y, big_z)
                start = pl.multiple_of(h * 2 * half + c * half, half)
                for s in range(4):

                    @pl.when(slot == s)
                    def _(s=s, j=j, start=start, piece=pieces[k * 2 + other]):
                        @pl.loop(0, rows // 128)
                        def _(r):
                            band = pl.ds(pl.multiple_of(r * 128, 128), 128)
                            outs[s][j, band, :] = piece[band, pl.ds(start, half)]


def second_pack_kernel(where, *refs):
    parts, outs = refs[:4], refs[4:8]
    rows = outs[0].shape[1] - EXTRA
    mine = jnp.where(where[3] == 0, where[1], where[0])
    tail = pl.ds(rows, EXTRA)
    for j in range(4):
        block = split_rows(sum(joined(part[j, tail, :]) for part in parts))
        for u in range(4):
            outs[u][j, tail, :] = block
    for u in range(4):
        j = lax.rem(mine + u, 4)
        for s in range(4):
            outs[u][s, 0:rows, :] = parts[s][j, 0:rows, :]


def pack_call(kernel, where, inputs, rows, half, name):
    vmem = pl.BlockSpec(memory_space=pltpu.VMEM)
    return pl.pallas_call(
        kernel,
        in_specs=[pl.BlockSpec(memory_space=pltpu.SMEM)] + [vmem] * len(inputs),
        out_specs=[vmem] * 4,
        out_shape=[jax.ShapeDtypeStruct((4, rows + EXTRA, half), BF)] * 4,
        compiler_params=pltpu.CompilerParams(vmem_limit_bytes=16 * 1024 * 1024),
        cost_estimate=pl.CostEstimate(
            flops=0, bytes_accessed=64 * rows * half, transcendentals=0
        ),
        name=name,
    )(where, *inputs)


def projection_kernel(members, first, last, where, gathered, *refs):
    count = sum(len(group) for group in members)
    parts = refs[:count]
    refs = refs[count:]
    before = None if first else refs[0]
    out = refs[2 if last else 0 if first else 1]
    if last:
        refs[3][...] = jnp.sum(refs[1][...], axis=0, keepdims=True)
    z, y, c = where[0], where[1], where[3]
    half = out.shape[-2] // (2 if last else 1)
    rows = parts[0].shape[1] - EXTRA
    used = 0
    for n in range(2):
        z_first = (c == 0) if n == 0 else (c == 1)
        total = None if first else before[n]
        for u in members[n]:
            part = parts[used]
            used += 1
            for s in range(4):
                dz, dy = jnp.where(z_first, s, u), jnp.where(z_first, u, s)
                row = lax.rem(z + 4 - dz, 4) * 4 + lax.rem(y + 4 - dy, 4)
                row = pl.multiple_of(row * rows, rows)
                term = lax.dot_general(
                    part[s, 0:rows, :],
                    gathered[pl.ds(row, rows), :],
                    (((0,), (0,)), ((), ())),
                    preferred_element_type=F32,
                )
                total = term if total is None else total + term
        if last:
            holder = c if n == 0 else 1 - c
            start = pl.multiple_of(holder * half, half)
            out[pl.ds(start, half), :] = total.astype(BF)
        else:
            out[n] = total


def projection_call(where, mine, theirs, gathered, members, before, tails=None):
    rows, half = mine[0].shape[1] - EXTRA, mine[0].shape[2]
    depth = gathered.shape[1]
    vmem = pl.BlockSpec(memory_space=pltpu.VMEM)
    picked = [mine[u] for u in members[0]] + [theirs[u] for u in members[1]]
    blocks = 4 * len(picked)
    first, last = before is None, tails is not None
    return pl.pallas_call(
        functools.partial(projection_kernel, members, first, last),
        in_specs=[pl.BlockSpec(memory_space=pltpu.SMEM), vmem]
        + [vmem] * len(picked)
        + ([] if first else [vmem])
        + ([vmem] if last else []),
        out_specs=[vmem, vmem] if last else vmem,
        out_shape=[
            jax.ShapeDtypeStruct((2 * half, depth), BF),
            jax.ShapeDtypeStruct((1, 4 * half), F32),
        ]
        if last
        else jax.ShapeDtypeStruct((2, half, depth), F32),
        compiler_params=pltpu.CompilerParams(vmem_limit_bytes=24 * 1024 * 1024),
        cost_estimate=pl.CostEstimate(
            flops=2 * blocks * rows * half * depth,
            bytes_accessed=2 * blocks * rows * (depth + half),
            transcendentals=0,
        ),
        name="projection_grad",
    )(where, gathered, *picked, *([] if first else [before]), *([tails] if last else []))


def local_stats(rewards, group_ids, kept_flags, lengths):
    kept = kept_flags.astype(F32)
    onehot = (group_ids[None, :] == jnp.arange(GROUPS, dtype=jnp.int32)[:, None]).astype(F32)
    values = [
        jnp.sum(onehot * kept[None, :], axis=1),
        jnp.sum(onehot * (kept * rewards)[None, :], axis=1),
        jnp.sum(onehot * (kept * rewards * rewards)[None, :], axis=1),
        jnp.sum(kept * lengths[0].astype(F32))[None],
        jnp.zeros((128 - 3 * GROUPS - 1,), F32),
    ]
    return jnp.concatenate(values)[None, :]


def token_info(rewards, group_ids, kept_flags, lengths, rows):
    ends = jnp.cumsum(lengths[0])
    position = jnp.arange(rows, dtype=jnp.int32)
    segment = jnp.sum((position[None, :] >= ends[:, None]).astype(jnp.int32), axis=0)
    picks = (segment[None, :] == jnp.arange(rewards.shape[0], dtype=jnp.int32)[:, None]).astype(F32)
    values = [rewards, kept_flags.astype(F32), group_ids.astype(F32)]
    found = [jnp.sum(picks * value[:, None], axis=0, keepdims=True) for value in values]
    return jnp.concatenate(found + [jnp.zeros((5, rows), F32)], axis=0)


def shards(
    attention, residual, out_proj, norm_gain, cotangent, rewards, group_ids, kept_flags, lengths
):
    rows = attention.shape[0]
    features = out_proj.shape[0]
    d, t = lax.axis_index("dp"), lax.axis_index("tensor")
    where = jnp.stack([d // 4, d % 4, t // 2, t % 2]).astype(jnp.int32)
    gain = norm_gain[None, :]

    arrived = {}
    send2, keep2, send1, send3 = partial_products(
        where,
        attention,
        out_proj,
        [(2, True, False, BF), (2, False, False, F32), (1, True, False, BF), (3, True, False, BF)],
    )
    gathered = lax.all_gather(attention, "dp", axis=0, tiled=True)
    width = features // 8
    top, bottom = small_call(
        halves_kernel, [keep2, swap(send2)], [(rows // 2, width)] * 2, "halves"
    )
    late_where, _, _ = lax.optimization_barrier((where, top, bottom))
    top = lax.ppermute(top, "tensor", x_shift(1))
    bottom = lax.ppermute(bottom, "tensor", x_shift(3))
    first, third, send0 = partial_products(
        late_where,
        attention,
        out_proj,
        [(1, False, True, F32), (3, False, True, F32), (0, True, False, BF)],
        [swap(send1), swap(send3)],
    )
    first, third = small_call(
        passed_kernel, [first, third, top, bottom], [(rows, width)] * 2, "passed"
    )
    arrived[1] = lax.ppermute(first, "tensor", x_shift(1))
    arrived[3] = lax.ppermute(third, "tensor", x_shift(3))
    stats = local_stats(rewards, group_ids, kept_flags, lengths)
    info = token_info(rewards, group_ids, kept_flags, lengths, rows)
    stats, info, _ = lax.optimization_barrier((stats, info, third))
    late_where, _ = lax.optimization_barrier((where, third))
    stats = [lax.ppermute(stats, ("dp", "tensor"), scattered(step)) for step in (0, 1)]
    (own,) = partial_products(
        late_where, attention, out_proj, [(0, False, True, F32)], [swap(send0)]
    )
    residual, info = lax.optimization_barrier((residual, info))
    hidden, sums = hidden_call(
        own, arrived[1], arrived[3], residual, cotangent, gain, *stats
    )

    chip = sums + swap(sums)
    others = [lax.ppermute(chip, "tensor", x_shift(k)) for k in (1, 2, 3)]
    tokens = rows * lax.axis_size("dp")
    grad_residual, own_piece, gain_term = grad_call(
        features, tokens, hidden, cotangent, gain, chip, *others, info
    )

    near = {k: lax.ppermute(own_piece, "tensor", x_shift(k)) for k in (1, 3)}
    top = lax.ppermute(near[1][: rows // 2], "tensor", x_shift(1))
    bottom = lax.ppermute(near[3][rows // 2 :], "tensor", x_shift(3))
    (far,) = small_call(joined_kernel, [top, bottom], [(rows, width)], "joined")
    pieces = []
    for piece in (own_piece, near[1], far, near[3]):
        pieces.extend([piece, swap(piece)])
    half = features // 32
    sends = pack_call(first_pack_kernel, where, pieces + [gain_term], rows, half, "first_pack")
    parts = {0: sends[0]}
    for k in (2, 1, 3):
        parts[k] = lax.ppermute(sends[k], ("dp", "tensor"), plane_shift(0, k))
    parts = [parts[k] for k in range(4)]
    late_where, _ = lax.optimization_barrier((where, sends))
    grad_attention = attention_call(late_where, pieces, out_proj)
    pack_where, _ = lax.optimization_barrier((where, grad_attention))
    sends = pack_call(second_pack_kernel, pack_where, parts, rows, half, "second_pack")
    mine = {0: sends[0]}
    for k in (2, 1, 3):
        mine[k] = lax.ppermute(sends[k], ("dp", "tensor"), plane_shift(1, k))
    theirs = [swap(mine[0]), None, None, None]
    total = projection_call(where, mine, theirs, gathered, ((0,), (0,)), None)
    for k in (1, 3, 2):
        mine[k], total = lax.optimization_barrier((mine[k], total))
        theirs[k] = swap(mine[k])
    total = projection_call(where, mine, theirs, gathered, ((1, 3, 2), ()), total)
    tails = sum(part[:, rows:, :].astype(F32) for part in mine.values())
    tails = jnp.concatenate([tails[j] for j in range(4)], axis=1)
    grad_out_proj, grad_gain = projection_call(
        where, mine, theirs, gathered, ((), (1, 3, 2)), total, tails
    )
    return (grad_attention, grad_out_proj, grad_residual, grad_gain[0])


def solution(mesh):
    return jax.shard_map(
        shards,
        mesh=mesh,
        in_specs=(
            P("dp", "tensor"),
            P("dp", "tensor"),
            P(None, "tensor"),
            P("tensor"),
            P("dp", "tensor"),
            P("dp"),
            P("dp"),
            P("dp"),
            P("dp", None),
        ),
        out_specs=(P("dp", "tensor"), P("dp", "tensor"), P("dp", "tensor"), P("tensor")),
        check_vma=False,
    )
```

```python
import functools

import jax
import jax.numpy as jnp
from jax import lax
from jax.experimental import pallas as pl
from jax.experimental.pallas import tpu as pltpu
from jax.sharding import PartitionSpec as P

BF = jnp.bfloat16
F32 = jnp.float32
LIMIT = 48 * 1024 * 1024
SMALL = 16 * 1024 * 1024
EXTRA = 16
GROUPS = 4
CORE_SWAP = [(t, t ^ 1) for t in range(8)]


def x_shift(k):
    return [(t, ((t // 2 + k) % 4) * 2 + t % 2) for t in range(8)]


def plane_shift(stage, k):
    pairs = []
    for d in range(16):
        for t in range(8):
            z, y = d // 4, d % 4
            if (t % 2) == stage:
                z = (z + k) % 4
            else:
                y = (y + k) % 4
            pairs.append((d * 8 + t, (z * 4 + y) * 8 + t))
    return pairs


def scattered(step):
    return [(d * 8 + t, ((d + 2 * t + step) % 16) * 8 + t) for d in range(16) for t in range(8)]


def swap(value):
    return lax.ppermute(value, "tensor", CORE_SWAP)


def params():
    return pltpu.CompilerParams(vmem_limit_bytes=LIMIT)


def partial_kernel(jobs, where, att, w, *refs):
    ins = sum(1 for job in jobs if job[2])
    got, outs = refs[:ins], refs[ins:-2]
    buf, sems = refs[-2:]
    x, c = where[2], where[3]
    step = buf.shape[1]
    copies = []
    for shift, other, _, _ in jobs:
        piece = lax.rem(x + shift, 4) * 2 + (1 - c if other else c)
        for h in range(2):
            row = pl.multiple_of((piece * 2 + h) * step, step)
            n = len(copies)
            copies.append(pltpu.make_async_copy(w.at[pl.ds(row, step)], buf.at[n], sems.at[n]))
    for copy in copies:
        copy.start()
    used = 0
    for n, (_, _, add, _) in enumerate(jobs):
        if add:
            used += 1

        for h in range(2):
            copies[2 * n + h].wait()

        @pl.loop(0, 2)
        def _(h, n=n, add=add, used=used):
            columns = pl.ds(pl.multiple_of(h * step, step), step)
            term = lax.dot_general(
                att[...], buf[2 * n + h], (((1,), (1,)), ((), ())), preferred_element_type=F32
            )
            if add:
                term += got[used - 1][:, columns].astype(F32)
            outs[n][:, columns] = term.astype(outs[n].dtype)


def partial_products(where, attention, out_proj, jobs, got=()):
    rows, depth = attention.shape
    width = out_proj.shape[0] // 8
    step = width // 2
    count = 2 * len(jobs)
    vmem = pl.BlockSpec(memory_space=pltpu.VMEM)
    far = pl.BlockSpec(memory_space=pltpu.HBM)
    return pl.pallas_call(
        functools.partial(partial_kernel, jobs),
        in_specs=[pl.BlockSpec(memory_space=pltpu.SMEM), vmem, far] + [vmem] * len(got),
        out_specs=[vmem] * len(jobs),
        out_shape=[jax.ShapeDtypeStruct((rows, width), job[3]) for job in jobs],
        scratch_shapes=[
            pltpu.VMEM((count, step, depth), BF),
            pltpu.SemaphoreType.DMA((count,)),
        ],
        compiler_params=params(),
        cost_estimate=pl.CostEstimate(
            flops=count * rows * depth * width,
            bytes_accessed=count * width * depth,
            transcendentals=0,
        ),
        name="partial",
    )(where, attention, out_proj, *got)


def halves_kernel(first, second, top, bottom):
    rows = top.shape[0]

    @pl.loop(0, rows // 64)
    def _(i):
        for n, out in ((0, top), (1, bottom)):
            band = pl.ds(pl.multiple_of(n * rows + i * 64, 64), 64)
            here = pl.ds(pl.multiple_of(i * 64, 64), 64)
            out[here, :] = (first[band, :] + second[band, :].astype(F32)).astype(BF)


def passed_kernel(first, third, top, bottom, next_first, next_third):
    rows = top.shape[0]

    @pl.loop(0, rows // 64)
    def _(i):
        low = pl.ds(pl.multiple_of(i * 64, 64), 64)
        high = pl.ds(pl.multiple_of(rows + i * 64, 64), 64)
        next_first[low, :] = (first[low, :] + top[low, :].astype(F32)).astype(BF)
        next_first[high, :] = first[high, :].astype(BF)
        next_third[low, :] = third[low, :].astype(BF)
        next_third[high, :] = (third[high, :] + bottom[low, :].astype(F32)).astype(BF)


def joined_kernel(top, bottom, out):
    rows = top.shape[0]

    @pl.loop(0, rows // 64)
    def _(i):
        low = pl.ds(pl.multiple_of(i * 64, 64), 64)
        high = pl.ds(pl.multiple_of(rows + i * 64, 64), 64)
        out[low, :] = top[low, :]
        out[high, :] = bottom[low, :]


def small_call(kernel, inputs, shapes, name):
    vmem = pl.BlockSpec(memory_space=pltpu.VMEM)
    return pl.pallas_call(
        kernel,
        in_specs=[vmem] * len(inputs),
        out_specs=[vmem] * len(shapes),
        out_shape=[jax.ShapeDtypeStruct(shape, BF) for shape in shapes],
        compiler_params=pltpu.CompilerParams(vmem_limit_bytes=SMALL),
        cost_estimate=pl.CostEstimate(
            flops=inputs[0].size, bytes_accessed=8 * inputs[0].size, transcendentals=0
        ),
        name=name,
    )(*inputs)


def row_sums(value):
    rows, width = value.shape
    part = value[:, 0:128]
    for i in range(1, width // 128):
        part = part + value[:, i * 128 : (i + 1) * 128]
    return jnp.sum(part.T, axis=0, keepdims=True)


def hidden_kernel(own, r1, r3, residual, cot, gain, even, odd, hidden, sums):
    @pl.loop(0, own.shape[0] // 128)
    def _(i):
        band = pl.ds(pl.multiple_of(i * 128, 128), 128)
        h = own[band, :] + residual[band, :].astype(F32)
        h = h + r1[band, :].astype(F32) + r3[band, :].astype(F32)
        hidden[band, :] = h
        scaled = cot[band, :].astype(F32) * gain[...].astype(F32)
        first = row_sums(h * h)
        second = row_sums(scaled * h)
        rest = [even[...] + odd[...], jnp.zeros((5, 128), F32)]
        sums[:, band] = jnp.concatenate([first, second] + rest, axis=0)


def hidden_call(own, r1, r3, residual, cot, gain, even, odd):
    rows, width = own.shape
    vmem = pl.BlockSpec(memory_space=pltpu.VMEM)
    return pl.pallas_call(
        hidden_kernel,
        in_specs=[vmem] * 8,
        out_specs=[vmem] * 2,
        out_shape=[
            jax.ShapeDtypeStruct((rows, width), F32),
            jax.ShapeDtypeStruct((8, rows), F32),
        ],
        compiler_params=pltpu.CompilerParams(vmem_limit_bytes=SMALL),
        cost_estimate=pl.CostEstimate(
            flops=12 * rows * width, bytes_accessed=20 * rows * width, transcendentals=0
        ),
        name="hidden",
    )(own, r1, r3, residual, cot, gain, even, odd)


def column(row):
    return jnp.broadcast_to(row, (128, 128)).T


def spread(col, width):
    return jnp.concatenate([col] * (width // 128), axis=1)


def split_rows(value):
    high = value.astype(BF)
    rest = value - high.astype(F32)
    middle = rest.astype(BF)
    low = (rest - middle.astype(F32)).astype(BF)
    empty = jnp.zeros((EXTRA - 3, value.shape[1]), F32)
    parts = [high.astype(F32), middle.astype(F32), low.astype(F32), empty]
    return jnp.concatenate(parts, axis=0).astype(BF)


def joined(block):
    return jnp.sum(block.astype(F32), axis=0, keepdims=True)


def grad_kernel(features, tokens, hidden, cot, gain, s0, s1, s2, s3, info, grad, piece, total):
    width = hidden.shape[1]
    total[...] = jnp.zeros_like(total)

    @pl.loop(0, hidden.shape[0] // 128)
    def _(i):
        band = pl.ds(pl.multiple_of(i * 128, 128), 128)
        sums = s0[:, band] + s1[:, band] + s2[:, band] + s3[:, band]
        square, inner = sums[0:1, :], sums[1:2, :]
        inverse = lax.rsqrt(square / features + 1e-06)
        reward, kept, group = info[0:1, band], info[1:2, band], info[2:3, band]

        def picked(offset):
            value = jnp.zeros_like(reward)
            for g in range(GROUPS):
                stat = jnp.broadcast_to(sums[2:3, offset + g : offset + g + 1], value.shape)
                value = jnp.where(group == float(g), stat, value)
            return value

        count = jnp.maximum(picked(0), 1.0)
        mean = picked(GROUPS) / count
        variance = picked(2 * GROUPS) / count - mean * mean
        advantage = (reward - mean) / jnp.sqrt(jnp.maximum(variance, 1.0))
        kept_tokens = jnp.broadcast_to(sums[2:3, 3 * GROUPS : 3 * GROUPS + 1], reward.shape)
        coef = -advantage * kept * tokens / jnp.maximum(kept_tokens, 1.0)
        first = spread(column(coef * inverse), width)
        second = spread(column(coef * (inverse * inverse * inverse * inner / features)), width)
        h = hidden[band, :]
        c = cot[band, :].astype(F32)
        value = (first * (c * gain[...].astype(F32)) - h * second).astype(BF)
        grad[band, :] = value
        piece[band, :] = value
        total[...] += jnp.sum(first * c * h, axis=0, keepdims=True)


def grad_call(features, tokens, hidden, cot, gain, s0, s1, s2, s3, info):
    rows, width = hidden.shape
    vmem = pl.BlockSpec(memory_space=pltpu.VMEM)
    return pl.pallas_call(
        functools.partial(grad_kernel, float(features), float(tokens)),
        in_specs=[vmem] * 8,
        out_specs=[vmem] * 3,
        out_shape=[
            jax.ShapeDtypeStruct((rows, width), BF),
            jax.ShapeDtypeStruct((rows, width), BF),
            jax.ShapeDtypeStruct((1, width), F32),
        ],
        compiler_params=pltpu.CompilerParams(vmem_limit_bytes=SMALL),
        cost_estimate=pl.CostEstimate(
            flops=12 * rows * width, bytes_accessed=8 * rows * width, transcendentals=0
        ),
        name="grad",
    )(hidden, cot, gain, s0, s1, s2, s3, info)


def attention_kernel(where, *refs):
    pieces, w, out, buf, acc, sems = refs[:8], refs[8], refs[9], refs[10], refs[11], refs[12]
    x, c = where[2], where[3]
    step = buf.shape[1]
    copies = []
    for n in range(8):
        holder = (1 - c) if n % 2 else c
        piece = lax.rem(x + 4 - n // 2, 4) * 2 + holder
        row = pl.multiple_of(piece * step, step)
        copies.append(pltpu.make_async_copy(w.at[pl.ds(row, step)], buf.at[n], sems.at[n]))
        copies[-1].start()
    for n in range(8):
        copies[n].wait()
        term = jnp.dot(pieces[n][...], buf[n], preferred_element_type=F32)
        if n == 0:
            acc[...] = term
        elif n < 7:
            acc[...] += term
        else:
            out[...] = (acc[...] + term).astype(BF)


def attention_call(where, pieces, out_proj):
    rows, width = pieces[0].shape
    depth = out_proj.shape[1]
    vmem = pl.BlockSpec(memory_space=pltpu.VMEM)
    return pl.pallas_call(
        attention_kernel,
        in_specs=[pl.BlockSpec(memory_space=pltpu.SMEM)]
        + [vmem] * 8
        + [pl.BlockSpec(memory_space=pltpu.HBM)],
        out_specs=vmem,
        scratch_shapes=[
            pltpu.VMEM((8, width, depth), BF),
            pltpu.VMEM((rows, depth), F32),
            pltpu.SemaphoreType.DMA((8,)),
        ],
        out_shape=jax.ShapeDtypeStruct((rows, depth), BF),
        compiler_params=params(),
        cost_estimate=pl.CostEstimate(
            flops=2 * rows * depth * width * 8,
            bytes_accessed=2 * 8 * width * depth,
            transcendentals=0,
        ),
        name="attention_grad",
    )(where, *pieces, out_proj)


def first_pack_kernel(where, *refs):
    pieces, gain, outs = refs[:8], refs[8], refs[9:13]
    z, y, x, c = where[0], where[1], where[2], where[3]
    half = outs[0].shape[2]
    rows = outs[0].shape[1] - EXTRA
    for j in range(4):
        block = split_rows(gain[:, j * half : (j + 1) * half])
        for s in range(4):
            outs[s][j, rows : rows + EXTRA, :] = block
    for k in range(4):
        big_z = lax.rem(x + 4 - k, 4)
        for other in range(2):
            holder = (1 - c) if other else c
            for h in range(2):
                big_y = 2 * holder + h
                slot = jnp.where(c == 0, lax.rem(big_z + 4 - z, 4), lax.rem(big_y + 4 - y, 4))
                j = jnp.where(c == 0, big_y, big_z)
                start = pl.multiple_of(h * 2 * half + c * half, half)
                for s in range(4):

                    @pl.when(slot == s)
                    def _(s=s, j=j, start=start, piece=pieces[k * 2 + other]):
                        @pl.loop(0, rows // 128)
                        def _(r):
                            band = pl.ds(pl.multiple_of(r * 128, 128), 128)
                            outs[s][j, band, :] = piece[band, pl.ds(start, half)]


def second_pack_kernel(where, *refs):
    parts, outs = refs[:4], refs[4:8]
    rows = outs[0].shape[1] - EXTRA
    mine = jnp.where(where[3] == 0, where[1], where[0])
    tail = pl.ds(rows, EXTRA)
    for j in range(4):
        block = split_rows(sum(joined(part[j, tail, :]) for part in parts))
        for u in range(4):
            outs[u][j, tail, :] = block
    for u in range(4):
        j = lax.rem(mine + u, 4)
        for s in range(4):
            outs[u][s, 0:rows, :] = parts[s][j, 0:rows, :]


def pack_call(kernel, where, inputs, rows, half, name):
    vmem = pl.BlockSpec(memory_space=pltpu.VMEM)
    return pl.pallas_call(
        kernel,
        in_specs=[pl.BlockSpec(memory_space=pltpu.SMEM)] + [vmem] * len(inputs),
        out_specs=[vmem] * 4,
        out_shape=[jax.ShapeDtypeStruct((4, rows + EXTRA, half), BF)] * 4,
        compiler_params=pltpu.CompilerParams(vmem_limit_bytes=16 * 1024 * 1024),
        cost_estimate=pl.CostEstimate(
            flops=0, bytes_accessed=64 * rows * half, transcendentals=0
        ),
        name=name,
    )(where, *inputs)


def projection_kernel(members, first, last, where, gathered, *refs):
    count = sum(len(group) for group in members)
    parts = refs[:count]
    refs = refs[count:]
    before = None if first else refs[0]
    out = refs[2 if last else 0 if first else 1]
    if last:
        refs[3][...] = jnp.sum(refs[1][...], axis=0, keepdims=True)
    z, y, c = where[0], where[1], where[3]
    half = out.shape[-2] // (2 if last else 1)
    rows = parts[0].shape[1] - EXTRA
    used = 0
    for n in range(2):
        z_first = (c == 0) if n == 0 else (c == 1)
        total = None if first else before[n]
        for u in members[n]:
            part = parts[used]
            used += 1
            for s in range(4):
                dz, dy = jnp.where(z_first, s, u), jnp.where(z_first, u, s)
                row = lax.rem(z + 4 - dz, 4) * 4 + lax.rem(y + 4 - dy, 4)
                row = pl.multiple_of(row * rows, rows)
                term = lax.dot_general(
                    part[s, 0:rows, :],
                    gathered[pl.ds(row, rows), :],
                    (((0,), (0,)), ((), ())),
                    preferred_element_type=F32,
                )
                total = term if total is None else total + term
        if last:
            holder = c if n == 0 else 1 - c
            start = pl.multiple_of(holder * half, half)
            out[pl.ds(start, half), :] = total.astype(BF)
        else:
            out[n] = total


def projection_call(where, mine, theirs, gathered, members, before, tails=None):
    rows, half = mine[0].shape[1] - EXTRA, mine[0].shape[2]
    depth = gathered.shape[1]
    vmem = pl.BlockSpec(memory_space=pltpu.VMEM)
    picked = [mine[u] for u in members[0]] + [theirs[u] for u in members[1]]
    blocks = 4 * len(picked)
    first, last = before is None, tails is not None
    return pl.pallas_call(
        functools.partial(projection_kernel, members, first, last),
        in_specs=[pl.BlockSpec(memory_space=pltpu.SMEM), vmem]
        + [vmem] * len(picked)
        + ([] if first else [vmem])
        + ([vmem] if last else []),
        out_specs=[vmem, vmem] if last else vmem,
        out_shape=[
            jax.ShapeDtypeStruct((2 * half, depth), BF),
            jax.ShapeDtypeStruct((1, 4 * half), F32),
        ]
        if last
        else jax.ShapeDtypeStruct((2, half, depth), F32),
        compiler_params=pltpu.CompilerParams(vmem_limit_bytes=24 * 1024 * 1024),
        cost_estimate=pl.CostEstimate(
            flops=2 * blocks * rows * half * depth,
            bytes_accessed=2 * blocks * rows * (depth + half),
            transcendentals=0,
        ),
        name="projection_grad",
    )(where, gathered, *picked, *([] if first else [before]), *([tails] if last else []))


def local_stats(rewards, group_ids, kept_flags, lengths):
    kept = kept_flags.astype(F32)
    onehot = (group_ids[None, :] == jnp.arange(GROUPS, dtype=jnp.int32)[:, None]).astype(F32)
    values = [
        jnp.sum(onehot * kept[None, :], axis=1),
        jnp.sum(onehot * (kept * rewards)[None, :], axis=1),
        jnp.sum(onehot * (kept * rewards * rewards)[None, :], axis=1),
        jnp.sum(kept * lengths[0].astype(F32))[None],
        jnp.zeros((128 - 3 * GROUPS - 1,), F32),
    ]
    return jnp.concatenate(values)[None, :]


def token_info(rewards, group_ids, kept_flags, lengths, rows):
    ends = jnp.cumsum(lengths[0])
    position = jnp.arange(rows, dtype=jnp.int32)
    segment = jnp.sum((position[None, :] >= ends[:, None]).astype(jnp.int32), axis=0)
    picks = (segment[None, :] == jnp.arange(rewards.shape[0], dtype=jnp.int32)[:, None]).astype(F32)
    values = [rewards, kept_flags.astype(F32), group_ids.astype(F32)]
    found = [jnp.sum(picks * value[:, None], axis=0, keepdims=True) for value in values]
    return jnp.concatenate(found + [jnp.zeros((5, rows), F32)], axis=0)


def shards(
    attention, residual, out_proj, norm_gain, cotangent, rewards, group_ids, kept_flags, lengths
):
    rows = attention.shape[0]
    features = out_proj.shape[0]
    d, t = lax.axis_index("dp"), lax.axis_index("tensor")
    where = jnp.stack([d // 4, d % 4, t // 2, t % 2]).astype(jnp.int32)
    gain = norm_gain[None, :]

    arrived = {}
    send2, keep2, send1, send3 = partial_products(
        where,
        attention,
        out_proj,
        [(2, True, False, BF), (2, False, False, F32), (1, True, False, BF), (3, True, False, BF)],
    )
    gathered = lax.all_gather(attention, "dp", axis=0, tiled=True)
    width = features // 8
    top, bottom = small_call(
        halves_kernel, [keep2, swap(send2)], [(rows // 2, width)] * 2, "halves"
    )
    late_where, _, _ = lax.optimization_barrier((where, top, bottom))
    top = lax.ppermute(top, "tensor", x_shift(1))
    bottom = lax.ppermute(bottom, "tensor", x_shift(3))
    first, third, send0 = partial_products(
        late_where,
        attention,
        out_proj,
        [(1, False, True, F32), (3, False, True, F32), (0, True, False, BF)],
        [swap(send1), swap(send3)],
    )
    first, third = small_call(
        passed_kernel, [first, third, top, bottom], [(rows, width)] * 2, "passed"
    )
    arrived[1] = lax.ppermute(first, "tensor", x_shift(1))
    arrived[3] = lax.ppermute(third, "tensor", x_shift(3))
    stats = local_stats(rewards, group_ids, kept_flags, lengths)
    info = token_info(rewards, group_ids, kept_flags, lengths, rows)
    stats, info, _ = lax.optimization_barrier((stats, info, third))
    late_where, _ = lax.optimization_barrier((where, third))
    stats = [lax.ppermute(stats, ("dp", "tensor"), scattered(step)) for step in (0, 1)]
    (own,) = partial_products(
        late_where, attention, out_proj, [(0, False, True, F32)], [swap(send0)]
    )
    residual, info = lax.optimization_barrier((residual, info))
    hidden, sums = hidden_call(
        own, arrived[1], arrived[3], residual, cotangent, gain, *stats
    )

    chip = sums + swap(sums)
    others = [lax.ppermute(chip, "tensor", x_shift(k)) for k in (1, 2, 3)]
    tokens = rows * lax.axis_size("dp")
    grad_residual, own_piece, gain_term = grad_call(
        features, tokens, hidden, cotangent, gain, chip, *others, info
    )

    near = {k: lax.ppermute(own_piece, "tensor", x_shift(k)) for k in (1, 3)}
    top = lax.ppermute(near[1][: rows // 2], "tensor", x_shift(1))
    bottom = lax.ppermute(near[3][rows // 2 :], "tensor", x_shift(3))
    (far,) = small_call(joined_kernel, [top, bottom], [(rows, width)], "joined")
    pieces = []
    for piece in (own_piece, near[1], far, near[3]):
        pieces.extend([piece, swap(piece)])
    half = features // 32
    sends = pack_call(first_pack_kernel, where, pieces + [gain_term], rows, half, "first_pack")
    parts = {0: sends[0]}
    for k in (2, 1, 3):
        parts[k] = lax.ppermute(sends[k], ("dp", "tensor"), plane_shift(0, k))
    parts = [parts[k] for k in range(4)]
    late_where, _ = lax.optimization_barrier((where, sends))
    grad_attention = attention_call(late_where, pieces, out_proj)
    pack_where, _ = lax.optimization_barrier((where, grad_attention))
    sends = pack_call(second_pack_kernel, pack_where, parts, rows, half, "second_pack")
    mine = {0: sends[0]}
    for k in (2, 1, 3):
        mine[k] = lax.ppermute(sends[k], ("dp", "tensor"), plane_shift(1, k))
    theirs = [swap(mine[0]), None, None, None]
    total = projection_call(where, mine, theirs, gathered, ((0,), (0,)), None)
    for k in (1, 3):
        mine[k], total = lax.optimization_barrier((mine[k], total))
        theirs[k] = swap(mine[k])
    total = projection_call(where, mine, theirs, gathered, ((1, 3), ()), total)
    mine[2], total = lax.optimization_barrier((mine[2], total))
    theirs[2] = swap(mine[2])
    tails = sum(part[:, rows:, :].astype(F32) for part in mine.values())
    tails = jnp.concatenate([tails[j] for j in range(4)], axis=1)
    total = projection_call(where, mine, theirs, gathered, ((2,), (1, 3)), total)
    grad_out_proj, grad_gain = projection_call(
        where, mine, theirs, gathered, ((), (2,)), total, tails
    )
    return (grad_attention, grad_out_proj, grad_residual, grad_gain[0])


def solution(mesh):
    return jax.shard_map(
        shards,
        mesh=mesh,
        in_specs=(
            P("dp", "tensor"),
            P("dp", "tensor"),
            P(None, "tensor"),
            P("tensor"),
            P("dp", "tensor"),
            P("dp"),
            P("dp"),
            P("dp"),
            P("dp", None),
        ),
        out_specs=(P("dp", "tensor"), P("dp", "tensor"), P("dp", "tensor"), P("tensor")),
        check_vma=False,
    )
```

```python
import functools

import jax
import jax.numpy as jnp
from jax import lax
from jax.experimental import pallas as pl
from jax.experimental.pallas import tpu as pltpu
from jax.sharding import PartitionSpec as P

BF = jnp.bfloat16
F32 = jnp.float32
LIMIT = 48 * 1024 * 1024
SMALL = 16 * 1024 * 1024
EXTRA = 16
GROUPS = 4
CORE_SWAP = [(t, t ^ 1) for t in range(8)]


def x_shift(k):
    return [(t, ((t // 2 + k) % 4) * 2 + t % 2) for t in range(8)]


def plane_shift(stage, k):
    pairs = []
    for d in range(16):
        for t in range(8):
            z, y = d // 4, d % 4
            if (t % 2) == stage:
                z = (z + k) % 4
            else:
                y = (y + k) % 4
            pairs.append((d * 8 + t, (z * 4 + y) * 8 + t))
    return pairs


def scattered(step):
    return [(d * 8 + t, ((d + 2 * t + step) % 16) * 8 + t) for d in range(16) for t in range(8)]


def swap(value):
    return lax.ppermute(value, "tensor", CORE_SWAP)


def params():
    return pltpu.CompilerParams(vmem_limit_bytes=LIMIT)


def partial_kernel(jobs, where, att, w, *refs):
    ins = sum(1 for job in jobs if job[2])
    got, outs = refs[:ins], refs[ins:-2]
    buf, sems = refs[-2:]
    x, c = where[2], where[3]
    step = buf.shape[1]
    copies = []
    for shift, other, _, _ in jobs:
        piece = lax.rem(x + shift, 4) * 2 + (1 - c if other else c)
        for h in range(2):
            row = pl.multiple_of((piece * 2 + h) * step, step)
            n = len(copies)
            copies.append(pltpu.make_async_copy(w.at[pl.ds(row, step)], buf.at[n], sems.at[n]))
    for copy in copies:
        copy.start()
    used = 0
    for n, (_, _, add, _) in enumerate(jobs):
        if add:
            used += 1

        for h in range(2):
            copies[2 * n + h].wait()

        @pl.loop(0, 2)
        def _(h, n=n, add=add, used=used):
            columns = pl.ds(pl.multiple_of(h * step, step), step)
            term = lax.dot_general(
                att[...], buf[2 * n + h], (((1,), (1,)), ((), ())), preferred_element_type=F32
            )
            if add:
                term += got[used - 1][:, columns].astype(F32)
            outs[n][:, columns] = term.astype(outs[n].dtype)


def partial_products(where, attention, out_proj, jobs, got=()):
    rows, depth = attention.shape
    width = out_proj.shape[0] // 8
    step = width // 2
    count = 2 * len(jobs)
    vmem = pl.BlockSpec(memory_space=pltpu.VMEM)
    far = pl.BlockSpec(memory_space=pltpu.HBM)
    return pl.pallas_call(
        functools.partial(partial_kernel, jobs),
        in_specs=[pl.BlockSpec(memory_space=pltpu.SMEM), vmem, far] + [vmem] * len(got),
        out_specs=[vmem] * len(jobs),
        out_shape=[jax.ShapeDtypeStruct((rows, width), job[3]) for job in jobs],
        scratch_shapes=[
            pltpu.VMEM((count, step, depth), BF),
            pltpu.SemaphoreType.DMA((count,)),
        ],
        compiler_params=params(),
        cost_estimate=pl.CostEstimate(
            flops=count * rows * depth * width,
            bytes_accessed=count * width * depth,
            transcendentals=0,
        ),
        name="partial",
    )(where, attention, out_proj, *got)


def halves_kernel(first, second, top, bottom):
    rows = top.shape[0]

    @pl.loop(0, rows // 64)
    def _(i):
        for n, out in ((0, top), (1, bottom)):
            band = pl.ds(pl.multiple_of(n * rows + i * 64, 64), 64)
            here = pl.ds(pl.multiple_of(i * 64, 64), 64)
            out[here, :] = (first[band, :] + second[band, :].astype(F32)).astype(BF)


def passed_kernel(low, value, half, out):
    rows = half.shape[0]

    @pl.loop(0, rows // 64)
    def _(i):
        here = pl.ds(pl.multiple_of(i * 64, 64), 64)
        added = pl.ds(pl.multiple_of((0 if low else rows) + i * 64, 64), 64)
        alone = pl.ds(pl.multiple_of((rows if low else 0) + i * 64, 64), 64)
        out[added, :] = (value[added, :] + half[here, :].astype(F32)).astype(BF)
        out[alone, :] = value[alone, :].astype(BF)


def joined_kernel(top, bottom, out):
    rows = top.shape[0]

    @pl.loop(0, rows // 64)
    def _(i):
        low = pl.ds(pl.multiple_of(i * 64, 64), 64)
        high = pl.ds(pl.multiple_of(rows + i * 64, 64), 64)
        out[low, :] = top[low, :]
        out[high, :] = bottom[low, :]


def small_call(kernel, inputs, shapes, name):
    vmem = pl.BlockSpec(memory_space=pltpu.VMEM)
    return pl.pallas_call(
        kernel,
        in_specs=[vmem] * len(inputs),
        out_specs=[vmem] * len(shapes),
        out_shape=[jax.ShapeDtypeStruct(shape, BF) for shape in shapes],
        compiler_params=pltpu.CompilerParams(vmem_limit_bytes=SMALL),
        cost_estimate=pl.CostEstimate(
            flops=inputs[0].size, bytes_accessed=8 * inputs[0].size, transcendentals=0
        ),
        name=name,
    )(*inputs)


def row_sums(value):
    rows, width = value.shape
    part = value[:, 0:128]
    for i in range(1, width // 128):
        part = part + value[:, i * 128 : (i + 1) * 128]
    return jnp.sum(part.T, axis=0, keepdims=True)


def hidden_kernel(own, r1, r3, residual, cot, gain, even, odd, hidden, sums):
    @pl.loop(0, own.shape[0] // 128)
    def _(i):
        band = pl.ds(pl.multiple_of(i * 128, 128), 128)
        h = own[band, :] + residual[band, :].astype(F32)
        h = h + r1[band, :].astype(F32) + r3[band, :].astype(F32)
        hidden[band, :] = h
        scaled = cot[band, :].astype(F32) * gain[...].astype(F32)
        first = row_sums(h * h)
        second = row_sums(scaled * h)
        rest = [even[...] + odd[...], jnp.zeros((5, 128), F32)]
        sums[:, band] = jnp.concatenate([first, second] + rest, axis=0)


def hidden_call(own, r1, r3, residual, cot, gain, even, odd):
    rows, width = own.shape
    vmem = pl.BlockSpec(memory_space=pltpu.VMEM)
    return pl.pallas_call(
        hidden_kernel,
        in_specs=[vmem] * 8,
        out_specs=[vmem] * 2,
        out_shape=[
            jax.ShapeDtypeStruct((rows, width), F32),
            jax.ShapeDtypeStruct((8, rows), F32),
        ],
        compiler_params=pltpu.CompilerParams(vmem_limit_bytes=SMALL),
        cost_estimate=pl.CostEstimate(
            flops=12 * rows * width, bytes_accessed=20 * rows * width, transcendentals=0
        ),
        name="hidden",
    )(own, r1, r3, residual, cot, gain, even, odd)


def column(row):
    return jnp.broadcast_to(row, (128, 128)).T


def spread(col, width):
    return jnp.concatenate([col] * (width // 128), axis=1)


def split_rows(value):
    high = value.astype(BF)
    rest = value - high.astype(F32)
    middle = rest.astype(BF)
    low = (rest - middle.astype(F32)).astype(BF)
    empty = jnp.zeros((EXTRA - 3, value.shape[1]), F32)
    parts = [high.astype(F32), middle.astype(F32), low.astype(F32), empty]
    return jnp.concatenate(parts, axis=0).astype(BF)


def joined(block):
    return jnp.sum(block.astype(F32), axis=0, keepdims=True)


def grad_kernel(features, tokens, hidden, cot, gain, s0, s1, s2, s3, info, grad, piece, total):
    width = hidden.shape[1]
    total[...] = jnp.zeros_like(total)

    @pl.loop(0, hidden.shape[0] // 128)
    def _(i):
        band = pl.ds(pl.multiple_of(i * 128, 128), 128)
        sums = s0[:, band] + s1[:, band] + s2[:, band] + s3[:, band]
        square, inner = sums[0:1, :], sums[1:2, :]
        inverse = lax.rsqrt(square / features + 1e-06)
        reward, kept, group = info[0:1, band], info[1:2, band], info[2:3, band]

        def picked(offset):
            value = jnp.zeros_like(reward)
            for g in range(GROUPS):
                stat = jnp.broadcast_to(sums[2:3, offset + g : offset + g + 1], value.shape)
                value = jnp.where(group == float(g), stat, value)
            return value

        count = jnp.maximum(picked(0), 1.0)
        mean = picked(GROUPS) / count
        variance = picked(2 * GROUPS) / count - mean * mean
        advantage = (reward - mean) / jnp.sqrt(jnp.maximum(variance, 1.0))
        kept_tokens = jnp.broadcast_to(sums[2:3, 3 * GROUPS : 3 * GROUPS + 1], reward.shape)
        coef = -advantage * kept * tokens / jnp.maximum(kept_tokens, 1.0)
        first = spread(column(coef * inverse), width)
        second = spread(column(coef * (inverse * inverse * inverse * inner / features)), width)
        h = hidden[band, :]
        c = cot[band, :].astype(F32)
        value = (first * (c * gain[...].astype(F32)) - h * second).astype(BF)
        grad[band, :] = value
        piece[band, :] = value
        total[...] += jnp.sum(first * c * h, axis=0, keepdims=True)


def grad_call(features, tokens, hidden, cot, gain, s0, s1, s2, s3, info):
    rows, width = hidden.shape
    vmem = pl.BlockSpec(memory_space=pltpu.VMEM)
    return pl.pallas_call(
        functools.partial(grad_kernel, float(features), float(tokens)),
        in_specs=[vmem] * 8,
        out_specs=[vmem] * 3,
        out_shape=[
            jax.ShapeDtypeStruct((rows, width), BF),
            jax.ShapeDtypeStruct((rows, width), BF),
            jax.ShapeDtypeStruct((1, width), F32),
        ],
        compiler_params=pltpu.CompilerParams(vmem_limit_bytes=SMALL),
        cost_estimate=pl.CostEstimate(
            flops=12 * rows * width, bytes_accessed=8 * rows * width, transcendentals=0
        ),
        name="grad",
    )(hidden, cot, gain, s0, s1, s2, s3, info)


def attention_kernel(where, *refs):
    pieces, w, out, buf, acc, sems = refs[:8], refs[8], refs[9], refs[10], refs[11], refs[12]
    x, c = where[2], where[3]
    step = buf.shape[1]
    copies = []
    for n in range(8):
        holder = (1 - c) if n % 2 else c
        piece = lax.rem(x + 4 - n // 2, 4) * 2 + holder
        row = pl.multiple_of(piece * step, step)
        copies.append(pltpu.make_async_copy(w.at[pl.ds(row, step)], buf.at[n], sems.at[n]))
        copies[-1].start()
    for n in range(8):
        copies[n].wait()
        term = jnp.dot(pieces[n][...], buf[n], preferred_element_type=F32)
        if n == 0:
            acc[...] = term
        elif n < 7:
            acc[...] += term
        else:
            out[...] = (acc[...] + term).astype(BF)


def attention_call(where, pieces, out_proj):
    rows, width = pieces[0].shape
    depth = out_proj.shape[1]
    vmem = pl.BlockSpec(memory_space=pltpu.VMEM)
    return pl.pallas_call(
        attention_kernel,
        in_specs=[pl.BlockSpec(memory_space=pltpu.SMEM)]
        + [vmem] * 8
        + [pl.BlockSpec(memory_space=pltpu.HBM)],
        out_specs=vmem,
        scratch_shapes=[
            pltpu.VMEM((8, width, depth), BF),
            pltpu.VMEM((rows, depth), F32),
            pltpu.SemaphoreType.DMA((8,)),
        ],
        out_shape=jax.ShapeDtypeStruct((rows, depth), BF),
        compiler_params=params(),
        cost_estimate=pl.CostEstimate(
            flops=2 * rows * depth * width * 8,
            bytes_accessed=2 * 8 * width * depth,
            transcendentals=0,
        ),
        name="attention_grad",
    )(where, *pieces, out_proj)


def first_pack_kernel(where, *refs):
    pieces, gain, outs = refs[:8], refs[8], refs[9:13]
    z, y, x, c = where[0], where[1], where[2], where[3]
    half = outs[0].shape[2]
    rows = outs[0].shape[1] - EXTRA
    for j in range(4):
        block = split_rows(gain[:, j * half : (j + 1) * half])
        for s in range(4):
            outs[s][j, rows : rows + EXTRA, :] = block
    for k in range(4):
        big_z = lax.rem(x + 4 - k, 4)
        for other in range(2):
            holder = (1 - c) if other else c
            for h in range(2):
                big_y = 2 * holder + h
                slot = jnp.where(c == 0, lax.rem(big_z + 4 - z, 4), lax.rem(big_y + 4 - y, 4))
                j = jnp.where(c == 0, big_y, big_z)
                start = pl.multiple_of(h * 2 * half + c * half, half)
                for s in range(4):

                    @pl.when(slot == s)
                    def _(s=s, j=j, start=start, piece=pieces[k * 2 + other]):
                        @pl.loop(0, rows // 128)
                        def _(r):
                            band = pl.ds(pl.multiple_of(r * 128, 128), 128)
                            outs[s][j, band, :] = piece[band, pl.ds(start, half)]


def second_pack_kernel(where, *refs):
    parts, outs = refs[:4], refs[4:8]
    rows = outs[0].shape[1] - EXTRA
    mine = jnp.where(where[3] == 0, where[1], where[0])
    tail = pl.ds(rows, EXTRA)
    for j in range(4):
        block = split_rows(sum(joined(part[j, tail, :]) for part in parts))
        for u in range(4):
            outs[u][j, tail, :] = block
    for u in range(4):
        j = lax.rem(mine + u, 4)
        for s in range(4):
            outs[u][s, 0:rows, :] = parts[s][j, 0:rows, :]


def pack_call(kernel, where, inputs, rows, half, name):
    vmem = pl.BlockSpec(memory_space=pltpu.VMEM)
    return pl.pallas_call(
        kernel,
        in_specs=[pl.BlockSpec(memory_space=pltpu.SMEM)] + [vmem] * len(inputs),
        out_specs=[vmem] * 4,
        out_shape=[jax.ShapeDtypeStruct((4, rows + EXTRA, half), BF)] * 4,
        compiler_params=pltpu.CompilerParams(vmem_limit_bytes=16 * 1024 * 1024),
        cost_estimate=pl.CostEstimate(
            flops=0, bytes_accessed=64 * rows * half, transcendentals=0
        ),
        name=name,
    )(where, *inputs)


def projection_kernel(members, first, last, where, gathered, *refs):
    count = sum(len(group) for group in members)
    parts = refs[:count]
    refs = refs[count:]
    before = None if first else refs[0]
    out = refs[2 if last else 0 if first else 1]
    if last:
        refs[3][...] = jnp.sum(refs[1][...], axis=0, keepdims=True)
    z, y, c = where[0], where[1], where[3]
    half = out.shape[-2] // (2 if last else 1)
    rows = parts[0].shape[1] - EXTRA
    used = 0
    for n in range(2):
        z_first = (c == 0) if n == 0 else (c == 1)
        total = None if first else before[n]
        for u in members[n]:
            part = parts[used]
            used += 1
            for s in range(4):
                dz, dy = jnp.where(z_first, s, u), jnp.where(z_first, u, s)
                row = lax.rem(z + 4 - dz, 4) * 4 + lax.rem(y + 4 - dy, 4)
                row = pl.multiple_of(row * rows, rows)
                term = lax.dot_general(
                    part[s, 0:rows, :],
                    gathered[pl.ds(row, rows), :],
                    (((0,), (0,)), ((), ())),
                    preferred_element_type=F32,
                )
                total = term if total is None else total + term
        if last:
            holder = c if n == 0 else 1 - c
            start = pl.multiple_of(holder * half, half)
            out[pl.ds(start, half), :] = total.astype(BF)
        else:
            out[n] = total


def projection_call(where, mine, theirs, gathered, members, before, tails=None):
    rows, half = mine[0].shape[1] - EXTRA, mine[0].shape[2]
    depth = gathered.shape[1]
    vmem = pl.BlockSpec(memory_space=pltpu.VMEM)
    picked = [mine[u] for u in members[0]] + [theirs[u] for u in members[1]]
    blocks = 4 * len(picked)
    first, last = before is None, tails is not None
    return pl.pallas_call(
        functools.partial(projection_kernel, members, first, last),
        in_specs=[pl.BlockSpec(memory_space=pltpu.SMEM), vmem]
        + [vmem] * len(picked)
        + ([] if first else [vmem])
        + ([vmem] if last else []),
        out_specs=[vmem, vmem] if last else vmem,
        out_shape=[
            jax.ShapeDtypeStruct((2 * half, depth), BF),
            jax.ShapeDtypeStruct((1, 4 * half), F32),
        ]
        if last
        else jax.ShapeDtypeStruct((2, half, depth), F32),
        compiler_params=pltpu.CompilerParams(vmem_limit_bytes=24 * 1024 * 1024),
        cost_estimate=pl.CostEstimate(
            flops=2 * blocks * rows * half * depth,
            bytes_accessed=2 * blocks * rows * (depth + half),
            transcendentals=0,
        ),
        name="projection_grad",
    )(where, gathered, *picked, *([] if first else [before]), *([tails] if last else []))


def local_stats(rewards, group_ids, kept_flags, lengths):
    kept = kept_flags.astype(F32)
    onehot = (group_ids[None, :] == jnp.arange(GROUPS, dtype=jnp.int32)[:, None]).astype(F32)
    values = [
        jnp.sum(onehot * kept[None, :], axis=1),
        jnp.sum(onehot * (kept * rewards)[None, :], axis=1),
        jnp.sum(onehot * (kept * rewards * rewards)[None, :], axis=1),
        jnp.sum(kept * lengths[0].astype(F32))[None],
        jnp.zeros((128 - 3 * GROUPS - 1,), F32),
    ]
    return jnp.concatenate(values)[None, :]


def token_info(rewards, group_ids, kept_flags, lengths, rows):
    ends = jnp.cumsum(lengths[0])
    position = jnp.arange(rows, dtype=jnp.int32)
    segment = jnp.sum((position[None, :] >= ends[:, None]).astype(jnp.int32), axis=0)
    picks = (segment[None, :] == jnp.arange(rewards.shape[0], dtype=jnp.int32)[:, None]).astype(F32)
    values = [rewards, kept_flags.astype(F32), group_ids.astype(F32)]
    found = [jnp.sum(picks * value[:, None], axis=0, keepdims=True) for value in values]
    return jnp.concatenate(found + [jnp.zeros((5, rows), F32)], axis=0)


def shards(
    attention, residual, out_proj, norm_gain, cotangent, rewards, group_ids, kept_flags, lengths
):
    rows = attention.shape[0]
    features = out_proj.shape[0]
    d, t = lax.axis_index("dp"), lax.axis_index("tensor")
    where = jnp.stack([d // 4, d % 4, t // 2, t % 2]).astype(jnp.int32)
    gain = norm_gain[None, :]

    arrived = {}
    send2, keep2, send1, send3 = partial_products(
        where,
        attention,
        out_proj,
        [(2, True, False, BF), (2, False, False, F32), (1, True, False, BF), (3, True, False, BF)],
    )
    gathered = lax.all_gather(attention, "dp", axis=0, tiled=True)
    width = features // 8
    top, bottom = small_call(
        halves_kernel, [keep2, swap(send2)], [(rows // 2, width)] * 2, "halves"
    )
    late_where, _, _ = lax.optimization_barrier((where, top, bottom))
    top = lax.ppermute(top, "tensor", x_shift(1))
    bottom = lax.ppermute(bottom, "tensor", x_shift(3))
    first, third, send0 = partial_products(
        late_where,
        attention,
        out_proj,
        [(1, False, True, F32), (3, False, True, F32), (0, True, False, BF)],
        [swap(send1), swap(send3)],
    )
    (first,) = small_call(
        functools.partial(passed_kernel, True), [first, top], [(rows, width)], "passed"
    )
    arrived[1] = lax.ppermute(first, "tensor", x_shift(1))
    (third,) = small_call(
        functools.partial(passed_kernel, False), [third, bottom], [(rows, width)], "passed"
    )
    arrived[3] = lax.ppermute(third, "tensor", x_shift(3))
    stats = local_stats(rewards, group_ids, kept_flags, lengths)
    info = token_info(rewards, group_ids, kept_flags, lengths, rows)
    stats, _ = lax.optimization_barrier((stats, third))
    late_where, _ = lax.optimization_barrier((where, third))
    stats = [lax.ppermute(stats, ("dp", "tensor"), scattered(step)) for step in (0, 1)]
    (own,) = partial_products(
        late_where, attention, out_proj, [(0, False, True, F32)], [swap(send0)]
    )
    residual, info = lax.optimization_barrier((residual, info))
    hidden, sums = hidden_call(
        own, arrived[1], arrived[3], residual, cotangent, gain, *stats
    )

    chip = sums + swap(sums)
    others = [lax.ppermute(chip, "tensor", x_shift(k)) for k in (2, 1, 3)]
    tokens = rows * lax.axis_size("dp")
    grad_residual, own_piece, gain_term = grad_call(
        features, tokens, hidden, cotangent, gain, chip, *others, info
    )

    near = {k: lax.ppermute(own_piece, "tensor", x_shift(k)) for k in (1, 3)}
    top = lax.ppermute(near[1][: rows // 2], "tensor", x_shift(1))
    bottom = lax.ppermute(near[3][rows // 2 :], "tensor", x_shift(3))
    (far,) = small_call(joined_kernel, [top, bottom], [(rows, width)], "joined")
    pieces = []
    for piece in (own_piece, near[1], far, near[3]):
        pieces.extend([piece, swap(piece)])
    half = features // 32
    sends = pack_call(first_pack_kernel, where, pieces + [gain_term], rows, half, "first_pack")
    parts = {0: sends[0]}
    for k in (2, 1, 3):
        parts[k] = lax.ppermute(sends[k], ("dp", "tensor"), plane_shift(0, k))
    parts = [parts[k] for k in range(4)]
    late_where, _ = lax.optimization_barrier((where, sends))
    grad_attention = attention_call(late_where, pieces, out_proj)
    pack_where, _ = lax.optimization_barrier((where, grad_attention))
    sends = pack_call(second_pack_kernel, pack_where, parts, rows, half, "second_pack")
    mine = {0: sends[0]}
    for k in (2, 1, 3):
        mine[k] = lax.ppermute(sends[k], ("dp", "tensor"), plane_shift(1, k))
    theirs = [swap(mine[0]), None, None, None]
    total = projection_call(where, mine, theirs, gathered, ((0,), (0,)), None)
    for k in (1, 3):
        mine[k], total = lax.optimization_barrier((mine[k], total))
        theirs[k] = swap(mine[k])
    total = projection_call(where, mine, theirs, gathered, ((1, 3), ()), total)
    mine[2], total = lax.optimization_barrier((mine[2], total))
    theirs[2] = swap(mine[2])
    tails = sum(part[:, rows:, :].astype(F32) for part in mine.values())
    tails = jnp.concatenate([tails[j] for j in range(4)], axis=1)
    total = projection_call(where, mine, theirs, gathered, ((2,), (1, 3)), total)
    grad_out_proj, grad_gain = projection_call(
        where, mine, theirs, gathered, ((), (2,)), total, tails
    )
    return (grad_attention, grad_out_proj, grad_residual, grad_gain[0])


def solution(mesh):
    return jax.shard_map(
        shards,
        mesh=mesh,
        in_specs=(
            P("dp", "tensor"),
            P("dp", "tensor"),
            P(None, "tensor"),
            P("tensor"),
            P("dp", "tensor"),
            P("dp"),
            P("dp"),
            P("dp"),
            P("dp", None),
        ),
        out_specs=(P("dp", "tensor"), P("dp", "tensor"), P("dp", "tensor"), P("tensor")),
        check_vma=False,
    )
```
